32 devices in a mesh: tm: 4 (over x, core), chan: 8 (over z, y).
Axes of the slice: x: 2, y: 2, z: 4, core: 2. Of those that a mesh axis runs over, the one named last changes fastest.
Arguments:
- strain_rate: bfloat16 [512, 12, 16384], P('chan', 'tm'), may hold values from -600 to 600
- fir_taps: bfloat16 [32], replicated, may hold values from -1 to 1
- source_channels: int32 [128], replicated, may hold values from 0 to 511
Outputs:
- correlations: float32 [128, 512, 1024], P(None, ('chan', 'tm'))
The draws below stay inside these ranges and needn't reach their ends.
Inputs may be any that keep to these rules, and one draw needn't show every extreme that they name: `source_channels`: repeats may occur.
All inputs are finite; a program needn't handle non-finite values.
Results may differ from the reference program's by a relative error of at most 0.0029.
Values may be sent and summed in bfloat16 or wider, within the bound.
No kernel may reach another device: no remote copies, remote signals or barrier semaphores. Data moves between devices by JAX's collectives and lax.ppermute only.
A program may use at most 192 MiB of HBM per device.

```python
import math
import jax
import jax.numpy as jnp
from jax import lax

CH_DEV = 64
WIN = 4096
TAPS = 32
NFREQ = 512
BANDW = 64
K_LO = 32
LAGS = 1024
SRC = 128
CH = 512
NW = 12
N_TM = 4


def draw_strain_rate(key, part):
    key = jax.random.fold_in(key, 11)
    key_chan, key_window, key_random = jax.random.split(key, 3)
    chan_scale = 10.0 ** jax.random.uniform(key_chan, (CH, 1, 1), jnp.float32)
    window_scale = 10.0 ** jax.random.uniform(key_window, (1, NW, 1), jnp.float32)
    values = jnp.clip(jax.random.normal(key_random, (CH, NW, 4 * WIN), jnp.float32), -6.0, 6.0)
    return (values * chan_scale * window_scale).astype(jnp.bfloat16)


def plant(values, own_key, smallest, top_value):
    index_at = [jax.random.randint(jax.random.fold_in(own_key, axis), (), 0, length) for axis, length in enumerate(values.shape)]
    longest = values.shape.index(max(values.shape))
    next_to = index_at[:longest] + [(index_at[longest] + 1) % values.shape[longest]] + index_at[longest + 1:]
    return values.at[tuple(index_at)].set(smallest).at[tuple(next_to)].set(top_value)


def normal_values(rng, extent, spread, limit, kind=jnp.bfloat16):
    return jnp.clip(spread * jax.random.normal(rng, extent, jnp.float32), -limit, limit).astype(kind)


def setup_inputs(seed: int = 0) -> dict:
    key_of = jax.random.split(jax.random.key(seed), 4)
    return {
        "strain_rate": draw_strain_rate(jax.random.fold_in(key_of[3], 71), 0),
        "fir_taps": normal_values(key_of[1], (TAPS,), TAPS ** -0.5, 1.0),
        "source_channels": plant(jax.random.randint(key_of[2], (SRC,), 0, CH), jax.random.fold_in(key_of[2], 1), 0, CH - 1).astype(jnp.int32),
    }


def forward_table(length, bins, first_bin):
    sample_index = lax.broadcasted_iota(jnp.int32, (length, bins), 0)
    bin_index = lax.broadcasted_iota(jnp.int32, (length, bins), 1) + first_bin
    phases = sample_index * bin_index % (2 * length)
    angles = phases.astype(jnp.float32) * (math.pi / length)
    return jnp.concatenate([jnp.cos(angles), -jnp.sin(angles)], axis=1)

def lag_table(bins, first_bin, length, lag_count):
    bin_index = lax.broadcasted_iota(jnp.int32, (bins, lag_count), 0) + first_bin
    lag_index = lax.broadcasted_iota(jnp.int32, (bins, lag_count), 1) - lag_count // 2 + 2 * length
    phases = bin_index * lag_index % (2 * length)
    angles = phases.astype(jnp.float32) * (math.pi / length)
    return jnp.concatenate([jnp.cos(angles), -jnp.sin(angles)], axis=0)

def whiten(records, fir_taps, table, bins, band_width):
    channels, windows, samples = records.shape
    length = samples // 4
    signal = records.reshape(channels * windows, 1, samples)
    kernel = fir_taps.reshape(1, 1, -1)
    decimated = lax.conv_general_dilated(signal, kernel, (4,), [(fir_taps.shape[0] - 1, 0)], preferred_element_type=jnp.float32)
    decimated = decimated.reshape(channels * windows, length)
    spectrum = jnp.dot(decimated, table, precision=lax.Precision.HIGHEST, preferred_element_type=jnp.float32)
    grouped = spectrum.reshape(channels * windows, 2, bins // band_width, band_width)
    band_power = lax.optimization_barrier(jnp.sum(grouped * grouped, axis=(1, 3), keepdims=True)) / band_width
    whitened = grouped * lax.rsqrt(band_power + 1e-06)
    return whitened.reshape(channels, windows, 2, bins).astype(jnp.bfloat16)

def cross_spectra(source_part, local_part):
    src_real = source_part[:, :, 0].astype(jnp.float32)
    src_imag = source_part[:, :, 1].astype(jnp.float32)
    loc_real = local_part[:, :, 0].astype(jnp.float32)
    loc_imag = local_part[:, :, 1].astype(jnp.float32)
    pattern = 'swk,cwk->sck'
    highest = lax.Precision.HIGHEST
    real_part = jnp.einsum(pattern, src_real, loc_real, precision=highest) + jnp.einsum(pattern, src_imag, loc_imag, precision=highest)
    imag_part = jnp.einsum(pattern, src_imag, loc_real, precision=highest) - jnp.einsum(pattern, src_real, loc_imag, precision=highest)
    return jnp.stack([real_part, imag_part], axis=2)

def correlate(cross_spec, table, window_total):
    sources, channels, _, bins = cross_spec.shape
    flattened = cross_spec.reshape(sources * channels, 2 * bins)
    result = jnp.dot(flattened, table, precision=lax.Precision.HIGHEST, preferred_element_type=jnp.float32)
    result = result * (1.0 / math.sqrt(bins * window_total))
    return result.reshape(sources, channels, table.shape[1])

def reference(strain_rate, fir_taps, source_channels):
    ftable = forward_table(WIN, NFREQ, K_LO)
    ltable = lag_table(NFREQ, K_LO, WIN, LAGS)
    blocks = strain_rate.reshape(CH // CH_DEV, CH_DEV, NW, 4 * WIN)
    spectra = lax.map(lambda piece: whiten(piece, fir_taps, ftable, NFREQ, BANDW), blocks)
    spectra = spectra.reshape(CH, NW, 2, NFREQ)
    source_part = spectra[source_channels]
    local_rows = CH_DEV // N_TM
    pieces = spectra.reshape(CH // local_rows, local_rows, NW, 2, NFREQ)

    def one_block(piece):
        return correlate(cross_spectra(source_part, piece), ltable, NW)
    result = lax.map(one_block, pieces)
    return jnp.transpose(result, (1, 0, 2, 3)).reshape(SRC, CH, LAGS)
```

```python
import functools
import math

import jax
import jax.numpy as jnp
import numpy as np
from jax import lax
from jax.experimental import pallas as pl
from jax.experimental.pallas import tpu as pltpu
from jax.sharding import PartitionSpec as P

WIN = 4096
NFREQ = 512
BANDW = 64
K_LO = 32
LAGS = 1024
TAPS = 32
SUB = 512
GROUP = 8
SPEC = 2 * NFREQ
FIR_OUT = 256
FIR_IN = 4 * FIR_OUT + 128
MIB = 1 << 20


def forward_constants():
    samples = np.arange(SUB)[:, None]
    bins = np.arange(NFREQ)[None, :] + K_LO
    angles = 2.0 * np.pi * ((samples * bins) % (2 * WIN)) / (2 * WIN)
    table = np.concatenate([np.cos(angles), -np.sin(angles)], axis=1)
    high = table.astype(jnp.bfloat16)
    low = (table - high.astype(np.float64)).astype(jnp.bfloat16)
    return np.concatenate([high, high, low], axis=0)


def lag_constant():
    group, part, inner = np.meshgrid(
        np.arange(NFREQ // GROUP), np.arange(2), np.arange(GROUP), indexing="ij"
    )
    bins = (group * GROUP + inner).reshape(-1, 1) + K_LO
    lags = np.arange(LAGS)[None, :] - LAGS // 2 + 2 * WIN
    angles = 2.0 * np.pi * ((bins * lags) % (2 * WIN)) / (2 * WIN)
    table = np.where(part.reshape(-1, 1) == 0, np.cos(angles), -np.sin(angles))
    return table.astype(jnp.bfloat16)


def dot(a, b):
    return jnp.dot(a, b, preferred_element_type=jnp.float32)


def dot_nt(a, b):
    return lax.dot_general(a, b, (((1,), (1,)), ((), ())), preferred_element_type=jnp.float32)


def dot_tn(a, b):
    return lax.dot_general(a, b, (((0,), (0,)), ((), ())), preferred_element_type=jnp.float32)


def split(x):
    high = x.astype(jnp.bfloat16)
    return high, (x - high.astype(jnp.float32)).astype(jnp.bfloat16)


def turn_values(shape):
    index = (lax.broadcasted_iota(jnp.int32, shape, 1) + K_LO) % 16
    real = jnp.zeros(shape, jnp.float32)
    imag = jnp.zeros(shape, jnp.float32)
    for i in range(16):
        real = jnp.where(index == i, math.cos(math.pi * i / 8), real)
        imag = jnp.where(index == i, -math.sin(math.pi * i / 8), imag)
    return real, imag


def factors(chan_count, tm_count):
    inner = 2 if chan_count <= 8 else 4
    return {"z": chan_count // inner, "y": inner, "x": tm_count // 2, "c": 2}


def moved(sizes, index, outer, inner, by_outer, by_inner):
    n_outer, n_inner = sizes[outer], sizes[inner]
    hi = lax.rem(lax.div(index, n_inner) + by_outer + n_outer, n_outer)
    lo = lax.rem(lax.rem(index, n_inner) + by_inner + n_inner, n_inner)
    return hi * n_inner + lo


def chan_at(sizes, by_z, by_y):
    return moved(sizes, lax.axis_index("chan"), "z", "y", by_z, by_y)


def tm_at(sizes, by_x, by_c):
    return moved(sizes, lax.axis_index("tm"), "x", "c", by_x, by_c)


def shifted(sizes, value, **by):
    if not any(by.values()):
        return value
    axis, outer, inner = ("chan", "z", "y") if set(by) <= {"z", "y"} else ("tm", "x", "c")
    n_outer, n_inner = sizes[outer], sizes[inner]
    pairs = []
    for index in range(n_outer * n_inner):
        hi = (index // n_inner + by.get(outer, 0)) % n_outer
        lo = (index % n_inner + by.get(inner, 0)) % n_inner
        pairs.append((index, hi * n_inner + lo))
    return lax.ppermute(value, axis, pairs)


def fir_kernel(x_hbm, fir_hbm, out_ref, x_ref, fir_ref, toeplitz, sems, *, windows):
    chans = x_ref.shape[0] // windows
    fetch_fir = pltpu.make_async_copy(fir_hbm, fir_ref, sems.at[windows])
    fetch_fir.start()
    fetches = []
    for w in range(windows):
        mine = pl.ds(w * chans, chans)
        fetches.append(pltpu.make_async_copy(x_hbm.at[mine], x_ref.at[mine], sems.at[w]))
        fetches[-1].start()
    in_index = lax.broadcasted_iota(jnp.int32, (256, 128), 0)
    out_index = lax.broadcasted_iota(jnp.int32, (256, 128), 1)
    tap = in_index - 4 * (out_index % TAPS) - 97
    small = jnp.zeros((256, 128), jnp.float32)
    fetch_fir.wait()
    taps = fir_ref[...].astype(jnp.float32)
    for j in range(TAPS):
        small = jnp.where(tap == j, taps[0:1, j : j + 1], small)
    slot = lax.broadcasted_iota(jnp.int32, (128, 128), 1) // TAPS
    for a in range(FIR_IN // 128):
        for n in range(FIR_OUT // 128):
            here = jnp.where(slot + n * (128 // TAPS) == a, small[:128], 0.0)
            here = jnp.where(slot + n * (128 // TAPS) == a - 1, small[128:], here)
            toeplitz[a * 128 : (a + 1) * 128, n * 128 : (n + 1) * 128] = here.astype(jnp.bfloat16)

    step = 4 * FIR_OUT
    per = SUB // FIR_OUT
    together = 4

    def work(pieces, mine, first):
        piece = dot(jnp.concatenate(pieces, axis=0), toeplitz[...])
        high, low = split(piece)
        for n in range(together):
            i = (first + n) // per
            at = (n % per) * FIR_OUT
            part = slice(n * chans, (n + 1) * chans)
            out_ref[i, mine, at : at + FIR_OUT] = high[part]
            out_ref[i, mine, SUB + at : SUB + at + FIR_OUT] = low[part]
            out_ref[i, mine, 2 * SUB + at : 2 * SUB + at + FIR_OUT] = high[part]

    for w in range(windows):
        mine = slice(w * chans, (w + 1) * chans)
        fetches[w].wait()
        pieces = [jnp.concatenate([jnp.zeros((chans, 128), jnp.bfloat16), x_ref[mine, :step]], axis=1)]
        for n in range(1, together):
            pieces.append(x_ref[mine, n * step - 128 : (n + 1) * step])
        work(pieces, mine, 0)

        def body(j, carry, mine=mine):
            pieces = []
            for n in range(together):
                first = pl.multiple_of((j * together + n) * step - 128, 128)
                pieces.append(x_ref[mine, pl.ds(first, step + 128)])
            work(pieces, mine, j * together)
            return carry

        lax.fori_loop(1, WIN // FIR_OUT // together, body, 0)


def whiten_kernel(part_ref, *refs, windows, sizes):
    tm_count = sizes["x"] * sizes["c"]
    bins_out = refs[: sizes["z"]]
    rows_out = refs[sizes["z"] : sizes["z"] + tm_count]
    bins_ref, rows_ref = refs[sizes["z"] + tm_count :]
    blocks, rows, _ = part_ref.shape
    chans = rows // windows
    width = bins_ref.shape[2]
    own = rows_ref.shape[2]
    quarters = NFREQ // 128
    turn_re, turn_im = turn_values((1, NFREQ))
    band_a = lax.broadcasted_iota(jnp.int32, (128, 128), 0) // BANDW
    band_b = lax.broadcasted_iota(jnp.int32, (128, 128), 1) // BANDW
    same_band = (band_a == band_b).astype(jnp.bfloat16)
    src = lax.broadcasted_iota(jnp.int32, (256, 256), 0)
    dst = lax.broadcasted_iota(jnp.int32, (256, 256), 1)
    wanted = (dst // (2 * GROUP)) * GROUP + dst % GROUP + 128 * ((dst // GROUP) % 2)
    order = (src == wanted).astype(jnp.bfloat16)
    for w in range(windows):
        mine = slice(w * chans, (w + 1) * chans)
        real = part_ref[blocks - 1, mine, :NFREQ]
        imag = part_ref[blocks - 1, mine, NFREQ:]
        for i in reversed(range(blocks - 1)):
            real, imag = (
                part_ref[i, mine, :NFREQ] + real * turn_re - imag * turn_im,
                part_ref[i, mine, NFREQ:] + real * turn_im + imag * turn_re,
            )
        re = jnp.concatenate([real[:, q * 128 : (q + 1) * 128] for q in range(quarters)], axis=0)
        im = jnp.concatenate([imag[:, q * 128 : (q + 1) * 128] for q in range(quarters)], axis=0)
        power = re * re + im * im
        p0, p1 = split(power)
        p2 = (power - p0.astype(jnp.float32) - p1.astype(jnp.float32)).astype(jnp.bfloat16)
        total = dot(jnp.concatenate([p0, p1, p2], axis=1), jnp.concatenate([same_band] * 3, axis=0))
        gain = lax.rsqrt(total * (1.0 / BANDW) + 1e-06)
        both = jnp.concatenate(
            [(re * gain).astype(jnp.bfloat16), (im * gain).astype(jnp.bfloat16)], axis=1
        )
        both = dot(both, order).astype(jnp.bfloat16)
        for q in range(quarters):
            part = both[q * chans : (q + 1) * chans]
            for n in range(max(1, 256 // width)):
                bins_ref[q * 256 // width + n, mine] = part[:, n * width : (n + 1) * width]
            for t in range(tm_count):
                rows_ref[t, w, :, q * 256 : (q + 1) * 256] = part[t * own : (t + 1) * own]
    for z in range(sizes["z"]):
        for y in range(sizes["y"]):
            bins_out[z][y] = bins_ref[chan_at(sizes, z, y)]
    for x in range(sizes["x"]):
        for c in range(sizes["c"]):
            rows_out[x * sizes["c"] + c][...] = rows_ref[tm_at(sizes, x, c)]


def whitened_spectra(strain, taps, sizes):
    chans, windows, samples = strain.shape
    rows = chans * windows
    chan_count = sizes["z"] * sizes["y"]
    tm_count = sizes["x"] * sizes["c"]
    width = SPEC // chan_count
    own = chans // tm_count
    x = jnp.transpose(strain, (1, 0, 2)).reshape(rows, samples)
    blocks = WIN // SUB
    filtered = pl.pallas_call(
        functools.partial(fir_kernel, windows=windows),
        in_specs=[pl.BlockSpec(memory_space=pl.ANY)] * 2,
        out_shape=jax.ShapeDtypeStruct((blocks, rows, 3 * SUB), jnp.bfloat16),
        scratch_shapes=[
            pltpu.VMEM((rows, samples), jnp.bfloat16),
            pltpu.VMEM((1, TAPS), jnp.bfloat16),
            pltpu.VMEM((FIR_IN, FIR_OUT), jnp.bfloat16),
            pltpu.SemaphoreType.DMA((windows + 1,)),
        ],
        compiler_params=pltpu.CompilerParams(vmem_limit_bytes=58 * MIB),
        name="fir",
    )(x, taps.reshape(1, TAPS))
    part = dot(filtered.reshape(blocks * rows, 3 * SUB), jnp.asarray(forward_constants()))
    outs = pl.pallas_call(
        functools.partial(whiten_kernel, windows=windows, sizes=sizes),
        out_shape=[jax.ShapeDtypeStruct((sizes["y"], rows, width), jnp.bfloat16)] * sizes["z"]
        + [jax.ShapeDtypeStruct((windows, own, SPEC), jnp.bfloat16)] * tm_count,
        scratch_shapes=[
            pltpu.VMEM((chan_count, rows, width), jnp.bfloat16),
            pltpu.VMEM((tm_count, windows, own, SPEC), jnp.bfloat16),
        ],
        compiler_params=pltpu.CompilerParams(vmem_limit_bytes=24 * MIB),
        name="whiten",
    )(part.reshape(blocks, rows, SPEC))
    return outs[: sizes["z"]], outs[sizes["z"] :]


def pick_kernel(channels_ref, *refs, windows, sizes):
    bins = refs[: sizes["z"]]
    outs = refs[sizes["z"] :]
    chans = bins[0].shape[1] // windows
    sources = channels_ref.shape[1]
    chosen = []
    for z in range(sizes["z"]):
        first = chan_at(sizes, -z, 0) * chans
        ids = lax.broadcasted_iota(jnp.int32, (chans, sources), 0) + first
        chosen.append((ids == channels_ref[...]).astype(jnp.bfloat16))
    chosen = jnp.concatenate(chosen, axis=0)
    for y in range(sizes["y"]):
        for w in range(windows):
            block = jnp.concatenate([b[y, w * chans : (w + 1) * chans, :] for b in bins], axis=0)
            outs[y][0, w] = dot_tn(block, chosen).astype(jnp.bfloat16)


def picked_sources(source_channels, bins, windows, sizes):
    sources = source_channels.shape[0]
    width = bins[0].shape[2]
    shape = (1, windows, width, sources)
    parts = pl.pallas_call(
        functools.partial(pick_kernel, windows=windows, sizes=sizes),
        out_shape=[jax.ShapeDtypeStruct(shape, jnp.bfloat16)] * sizes["y"],
        compiler_params=pltpu.CompilerParams(vmem_limit_bytes=16 * MIB),
        name="pick",
    )(source_channels.reshape(1, sources), *bins)
    total = parts[0]
    for y in range(1, sizes["y"]):
        total = total + shifted(sizes, parts[y], y=y)
    return total


def block_at(sizes, step, sign):
    if sizes is None:
        return step
    z = lax.div(step, sizes["y"])
    y = lax.rem(step, sizes["y"])
    return chan_at(sizes, sign * z, sign * y)


def expand_kernel(*refs, sizes):
    out_ref = refs[-1]
    windows, own, _ = refs[0].shape
    depth = windows * (len(refs) - 1) * 2 * GROUP
    groups = 128 // (2 * GROUP)
    lane = lax.broadcasted_iota(jnp.int32, (own, 128), 1)
    first = lane % (2 * GROUP) < GROUP
    bin_row = lax.broadcasted_iota(jnp.int32, (own, GROUP, depth), 1)
    bin_lane = lax.broadcasted_iota(jnp.int32, (own, GROUP, depth), 2) % GROUP
    same = bin_row == bin_lane

    def body(step, carry):
        lanes = pl.ds(pl.multiple_of(block_at(sizes, step, -1) * 128, 128), 128)
        plain = []
        swapped = []
        for ref in refs[:-1]:
            for w in range(windows):
                x = ref[w, :, lanes].astype(jnp.float32)
                plain.append(x)
                ahead = pltpu.roll(x, 128 - GROUP, 1)
                behind = pltpu.roll(x, GROUP, 1)
                swapped.append(jnp.where(first, -ahead, behind))
        for g in range(groups):
            at = slice(g * 2 * GROUP, (g + 1) * 2 * GROUP)
            for p, parts in enumerate((plain, swapped)):
                a = jnp.concatenate([x[:, at] for x in parts], axis=1)
                full = jnp.where(same, a[:, None, :], 0.0)
                out_ref[step * groups + g, :, p * GROUP : (p + 1) * GROUP, :] = full.astype(jnp.bfloat16)
        return carry

    lax.fori_loop(0, SPEC // 128, body, 0)


def expanded_local(local, sizes):
    windows, own, _ = local[0].shape
    depth = windows * len(local) * 2 * GROUP
    out = pl.pallas_call(
        functools.partial(expand_kernel, sizes=sizes),
        out_shape=jax.ShapeDtypeStruct((SPEC // (2 * GROUP), own, 2 * GROUP, depth), jnp.bfloat16),
        cost_estimate=pl.CostEstimate(flops=4 * 10**9, bytes_accessed=8 * MIB, transcendentals=0),
        compiler_params=pltpu.CompilerParams(vmem_limit_bytes=24 * MIB),
        name="expand",
    )(*local)
    return out.reshape(SPEC // (2 * GROUP), own * 2 * GROUP, depth)


def cross_kernel(local_ref, *refs, fetch, own, sizes, by_y, aliased):
    sources = refs[: len(refs) - 2 - aliased]
    out_ref, wide = refs[-2:]
    count = sources[0].shape[-1]
    groups = 128 // (2 * GROUP)
    row = lax.broadcasted_iota(jnp.int32, (count, count), 0)
    column = lax.broadcasted_iota(jnp.int32, (count, count), 1)
    identity = (row == column).astype(jnp.bfloat16)

    def body(index, carry):
        step = index if by_y is None else index * sizes["y"] + by_y
        tiles = fetch(sources, step)
        cross = []
        for g in range(groups):
            rows = slice(g * 2 * GROUP, (g + 1) * 2 * GROUP)
            block = jnp.concatenate([tile[rows] for tile in tiles], axis=0)
            cross.append(dot(local_ref[step * groups + g], block).astype(jnp.bfloat16))
        tall = jnp.concatenate(
            [x[c * 2 * GROUP : (c + 1) * 2 * GROUP] for c in range(own) for x in cross], axis=0
        )
        turned = dot_nt(identity, tall)
        for c in range(own):
            wide[pl.ds(c, count, stride=own), :] = turned[:, c * 128 : (c + 1) * 128]
        lanes = pl.ds(pl.multiple_of(block_at(sizes, step, -1) * 128, 128), 128)
        out_ref[:, lanes] = wide[...].astype(jnp.bfloat16)
        return carry

    lax.fori_loop(0, SPEC // 128 if by_y is None else sizes["z"], body, 0)


def crossed(local, sources, fetch, sizes, by_y=None, held=None):
    _, expanded_rows, _ = local.shape
    own = expanded_rows // (2 * GROUP)
    count = sources[0].shape[-1]
    shape = jax.ShapeDtypeStruct((count * own, SPEC), jnp.bfloat16)
    extra = [] if held is None else [held]
    specs = [pl.BlockSpec(memory_space=pltpu.VMEM)] * (1 + len(sources))
    return pl.pallas_call(
        functools.partial(
            cross_kernel, fetch=fetch, own=own, sizes=sizes, by_y=by_y, aliased=len(extra)
        ),
        in_specs=specs + [pl.BlockSpec(memory_space=pltpu.VMEM)] * len(extra),
        out_shape=shape,
        input_output_aliases={1 + len(sources): 0} if extra else {},
        scratch_shapes=[pltpu.VMEM((count * own, 128), jnp.float32)],
        cost_estimate=pl.CostEstimate(flops=4 * 10**9, bytes_accessed=8 * MIB, transcendentals=0),
        compiler_params=pltpu.CompilerParams(vmem_limit_bytes=32 * MIB),
        name="cross",
    )(local, *sources, *extra)


def lag_kernel(cross_ref, table_ref, out_hbm, buffer, sems, *, scale):
    depth, height, lags = buffer.shape
    steps = cross_ref.shape[0] // height

    def store(i):
        mine = pl.ds(pl.multiple_of(i * height, height), height)
        slot = lax.rem(i, depth)
        return pltpu.make_async_copy(buffer.at[slot], out_hbm.at[mine], sems.at[slot])

    def body(i, carry):
        @pl.when(i >= depth)
        def _():
            store(i - depth).wait()

        rows = cross_ref[pl.ds(pl.multiple_of(i * height, height), height)]
        slot = lax.rem(i, depth)
        for n in range(lags // 256):
            at = slice(n * 256, (n + 1) * 256)
            buffer[slot, :, at] = dot(rows, table_ref[:, at]) * scale
        store(i).start()
        return carry

    lax.fori_loop(0, steps, body, 0)
    for i in range(max(0, steps - depth), steps):
        store(i).wait()


def correlations(cross, source_count, window_total):
    rows = cross.shape[0]
    height = 512
    out = pl.pallas_call(
        functools.partial(lag_kernel, scale=1.0 / math.sqrt(NFREQ * window_total)),
        in_specs=[pl.BlockSpec(memory_space=pltpu.VMEM)] * 2,
        out_specs=pl.BlockSpec(memory_space=pl.ANY),
        out_shape=jax.ShapeDtypeStruct((rows, LAGS), jnp.float32),
        scratch_shapes=[
            pltpu.VMEM((2, height, LAGS), jnp.float32),
            pltpu.SemaphoreType.DMA((2,)),
        ],
        compiler_params=pltpu.CompilerParams(vmem_limit_bytes=24 * MIB),
        name="lags",
    )(cross, jnp.asarray(lag_constant()))
    return out.reshape(source_count, -1, LAGS)


def gathered(picked, local, sizes):
    windows, width = picked.shape[1:3]
    half = width // 2
    whole = jnp.concatenate([shifted(sizes, picked, z=d) for d in range(sizes["z"])], axis=0)
    held = {(0, 0): [whole]}
    for x in range(1, sizes["x"]):
        held[x, 0] = [shifted(sizes, whole, x=x)]
    for y in range(1, sizes["y"]):
        held[0, y] = [shifted(sizes, whole, y=y)]
    expanded = expanded_local(local, sizes)
    edges = {key: array for key, array in held.items() if key != (0, 0)}
    edges, expanded = lax.optimization_barrier((edges, expanded))
    held.update(edges)
    for x in range(1, sizes["x"]):
        for y in range(1, sizes["y"]):
            held[x, y] = [
                shifted(sizes, held[0, y][0][:, :, :half], x=x),
                shifted(sizes, held[x, 0][0][:, :, half:], y=y),
            ]

    def rows_of(y):
        arrays = []
        place = {}
        for x in range(sizes["x"]):
            for c in range(sizes["c"]):
                place[x, c] = len(arrays)
                arrays += [shifted(sizes, array, c=c) for array in held[x, y]]

        def fetch(refs, step):
            by_z = lax.div(step, sizes["y"])
            tiles = []
            for x in range(sizes["x"]):
                for c in range(sizes["c"]):
                    parts = refs[place[x, c] : place[x, c] + len(held[x, y])]
                    for w in range(windows):
                        tiles.append(jnp.concatenate([part[by_z, w] for part in parts], axis=0))
            return tiles

        return arrays, fetch

    cross = None
    for y in range(sizes["y"]):
        if y > 0:
            far = {key: array for key, array in held.items() if key[0] and key[1]}
            far, cross = lax.optimization_barrier((far, cross))
            held.update(far)
        arrays, fetch = rows_of(y)
        cross = crossed(expanded, arrays, fetch, sizes, by_y=y, held=cross)
    return cross


def gathered_plainly(picked, local, sizes):
    parts = [shifted(sizes, picked, x=x, c=c) for x in range(sizes["x"]) for c in range(sizes["c"])]
    mine = jnp.concatenate(parts, axis=1)[0]
    total, width, count = mine.shape
    held = lax.all_gather(mine, "chan", axis=0, tiled=False)
    held = held.reshape(SPEC // 128, 128 // width, total, width, count)
    held = jnp.transpose(held, (0, 2, 1, 3, 4)).reshape(SPEC // 128, total, 128, count)

    def fetch(refs, step):
        return [refs[0][step, i] for i in range(total)]

    return crossed(expanded_local(local, None), [held], fetch, None)


def on_device(strain_rate, fir_taps, source_channels):
    sizes = factors(lax.axis_size("chan"), lax.axis_size("tm"))
    windows = strain_rate.shape[1]
    bins, rows = whitened_spectra(strain_rate, fir_taps, sizes)
    bins = [shifted(sizes, b, z=z) for z, b in enumerate(bins)]
    moves = [(x, c) for x in range(sizes["x"]) for c in range(sizes["c"])]
    local = [shifted(sizes, r, x=x, c=c) for r, (x, c) in zip(rows, moves)]
    bins, local = lax.optimization_barrier((bins, local))
    picked = picked_sources(source_channels, bins, windows, sizes)
    gather = gathered if picked.shape[2] == 128 else gathered_plainly
    cross = gather(picked, local, sizes)
    return correlations(cross, source_channels.shape[0], windows * lax.axis_size("tm"))


def solution(mesh):
    placed = (P("chan", "tm", None), P(), P())
    return jax.shard_map(
        on_device,
        mesh=mesh,
        in_specs=placed,
        out_specs=P(None, ("chan", "tm"), None),
        check_vma=False,
    )
```

```python
import functools
import math

import jax
import jax.numpy as jnp
import numpy as np
from jax import lax
from jax.experimental import pallas as pl
from jax.experimental.pallas import tpu as pltpu
from jax.sharding import PartitionSpec as P

WIN = 4096
NFREQ = 512
BANDW = 64
K_LO = 32
LAGS = 1024
TAPS = 32
SUB = 512
GROUP = 8
SPEC = 2 * NFREQ
FIR_OUT = 256
FIR_IN = 4 * FIR_OUT + 128
MIB = 1 << 20


def forward_constants():
    samples = np.arange(SUB)[:, None]
    bins = np.arange(NFREQ)[None, :] + K_LO
    angles = 2.0 * np.pi * ((samples * bins) % (2 * WIN)) / (2 * WIN)
    table = np.concatenate([np.cos(angles), -np.sin(angles)], axis=1)
    high = table.astype(jnp.bfloat16)
    low = (table - high.astype(np.float64)).astype(jnp.bfloat16)
    return np.concatenate([high, high, low], axis=0)


def lag_constant():
    group, part, inner = np.meshgrid(
        np.arange(NFREQ // GROUP), np.arange(2), np.arange(GROUP), indexing="ij"
    )
    bins = (group * GROUP + inner).reshape(-1, 1) + K_LO
    lags = np.arange(LAGS)[None, :] - LAGS // 2 + 2 * WIN
    angles = 2.0 * np.pi * ((bins * lags) % (2 * WIN)) / (2 * WIN)
    table = np.where(part.reshape(-1, 1) == 0, np.cos(angles), -np.sin(angles))
    return table.astype(jnp.bfloat16)


def dot(a, b):
    return jnp.dot(a, b, preferred_element_type=jnp.float32)


def dot_nt(a, b):
    return lax.dot_general(a, b, (((1,), (1,)), ((), ())), preferred_element_type=jnp.float32)


def dot_tn(a, b):
    return lax.dot_general(a, b, (((0,), (0,)), ((), ())), preferred_element_type=jnp.float32)


def split(x):
    high = x.astype(jnp.bfloat16)
    return high, (x - high.astype(jnp.float32)).astype(jnp.bfloat16)


def turn_values(shape):
    index = (lax.broadcasted_iota(jnp.int32, shape, 1) + K_LO) % 16
    real = jnp.zeros(shape, jnp.float32)
    imag = jnp.zeros(shape, jnp.float32)
    for i in range(16):
        real = jnp.where(index == i, math.cos(math.pi * i / 8), real)
        imag = jnp.where(index == i, -math.sin(math.pi * i / 8), imag)
    return real, imag


def factors(chan_count, tm_count):
    inner = 2 if chan_count <= 8 else 4
    return {"z": chan_count // inner, "y": inner, "x": tm_count // 2, "c": 2}


def moved(sizes, index, outer, inner, by_outer, by_inner):
    n_outer, n_inner = sizes[outer], sizes[inner]
    hi = lax.rem(lax.div(index, n_inner) + by_outer + n_outer, n_outer)
    lo = lax.rem(lax.rem(index, n_inner) + by_inner + n_inner, n_inner)
    return hi * n_inner + lo


def chan_at(sizes, by_z, by_y):
    return moved(sizes, lax.axis_index("chan"), "z", "y", by_z, by_y)


def tm_at(sizes, by_x, by_c):
    return moved(sizes, lax.axis_index("tm"), "x", "c", by_x, by_c)


def shifted(sizes, value, **by):
    if not any(by.values()):
        return value
    axis, outer, inner = ("chan", "z", "y") if set(by) <= {"z", "y"} else ("tm", "x", "c")
    n_outer, n_inner = sizes[outer], sizes[inner]
    pairs = []
    for index in range(n_outer * n_inner):
        hi = (index // n_inner + by.get(outer, 0)) % n_outer
        lo = (index % n_inner + by.get(inner, 0)) % n_inner
        pairs.append((index, hi * n_inner + lo))
    return lax.ppermute(value, axis, pairs)


def filter_matrix(taps, toeplitz):
    in_index = lax.broadcasted_iota(jnp.int32, (256, 128), 0)
    out_index = lax.broadcasted_iota(jnp.int32, (256, 128), 1)
    tap = in_index - 4 * (out_index % TAPS) - 97
    small = jnp.zeros((256, 128), jnp.float32)
    for j in range(TAPS):
        small = jnp.where(tap == j, taps[0:1, j : j + 1], small)
    slot = lax.broadcasted_iota(jnp.int32, (128, 128), 1) // TAPS
    for a in range(FIR_IN // 128):
        for n in range(FIR_OUT // 128):
            here = jnp.where(slot + n * (128 // TAPS) == a, small[:128], 0.0)
            here = jnp.where(slot + n * (128 // TAPS) == a - 1, small[128:], here)
            toeplitz[a * 128 : (a + 1) * 128, n * 128 : (n + 1) * 128] = here.astype(jnp.bfloat16)


def fir_kernel(x_hbm, fir_hbm, out_ref, x_ref, fir_ref, toeplitz, sems, *, windows):
    chans = x_ref.shape[0] // windows
    fetch_fir = pltpu.make_async_copy(fir_hbm, fir_ref, sems.at[windows])
    fetch_fir.start()
    fetches = []
    for w in range(windows):
        mine = pl.ds(w * chans, chans)
        fetches.append(pltpu.make_async_copy(x_hbm.at[mine], x_ref.at[mine], sems.at[w]))
        fetches[-1].start()
    fetch_fir.wait()
    filter_matrix(fir_ref[...].astype(jnp.float32), toeplitz)
    step = 4 * FIR_OUT
    per = SUB // FIR_OUT
    together = 4

    def work(pieces, mine, first):
        piece = dot(jnp.concatenate(pieces, axis=0), toeplitz[...])
        high, low = split(piece)
        for n in range(together):
            i = (first + n) // per
            at = (n % per) * FIR_OUT
            part = slice(n * chans, (n + 1) * chans)
            out_ref[i, mine, at : at + FIR_OUT] = high[part]
            out_ref[i, mine, SUB + at : SUB + at + FIR_OUT] = low[part]
            out_ref[i, mine, 2 * SUB + at : 2 * SUB + at + FIR_OUT] = high[part]

    for w in range(windows):
        mine = slice(w * chans, (w + 1) * chans)
        fetches[w].wait()
        pieces = [jnp.concatenate([jnp.zeros((chans, 128), jnp.bfloat16), x_ref[mine, :step]], axis=1)]
        for n in range(1, together):
            pieces.append(x_ref[mine, n * step - 128 : (n + 1) * step])
        work(pieces, mine, 0)

        def body(j, carry, mine=mine):
            pieces = []
            for n in range(together):
                first = pl.multiple_of((j * together + n) * step - 128, 128)
                pieces.append(x_ref[mine, pl.ds(first, step + 128)])
            work(pieces, mine, j * together)
            return carry

        lax.fori_loop(1, WIN // FIR_OUT // together, body, 0)


def whiten_kernel(part_ref, *refs, windows, sizes):
    tm_count = sizes["x"] * sizes["c"]
    bins_out = refs[: sizes["z"]]
    rows_out = refs[sizes["z"] : sizes["z"] + tm_count]
    bins_ref, rows_ref = refs[sizes["z"] + tm_count :]
    blocks, rows, _ = part_ref.shape
    chans = rows // windows
    width = bins_ref.shape[2]
    own = rows_ref.shape[2]
    quarters = NFREQ // 128
    turn_re, turn_im = turn_values((1, NFREQ))
    band_a = lax.broadcasted_iota(jnp.int32, (128, 128), 0) // BANDW
    band_b = lax.broadcasted_iota(jnp.int32, (128, 128), 1) // BANDW
    same_band = (band_a == band_b).astype(jnp.bfloat16)
    src = lax.broadcasted_iota(jnp.int32, (256, 256), 0)
    dst = lax.broadcasted_iota(jnp.int32, (256, 256), 1)
    wanted = (dst // (2 * GROUP)) * GROUP + dst % GROUP + 128 * ((dst // GROUP) % 2)
    order = (src == wanted).astype(jnp.bfloat16)
    for w in range(windows):
        mine = slice(w * chans, (w + 1) * chans)
        real = part_ref[blocks - 1, mine, :NFREQ]
        imag = part_ref[blocks - 1, mine, NFREQ:]
        for i in reversed(range(blocks - 1)):
            real, imag = (
                part_ref[i, mine, :NFREQ] + real * turn_re - imag * turn_im,
                part_ref[i, mine, NFREQ:] + real * turn_im + imag * turn_re,
            )
        re = jnp.concatenate([real[:, q * 128 : (q + 1) * 128] for q in range(quarters)], axis=0)
        im = jnp.concatenate([imag[:, q * 128 : (q + 1) * 128] for q in range(quarters)], axis=0)
        power = re * re + im * im
        p0, p1 = split(power)
        p2 = (power - p0.astype(jnp.float32) - p1.astype(jnp.float32)).astype(jnp.bfloat16)
        total = dot(jnp.concatenate([p0, p1, p2], axis=1), jnp.concatenate([same_band] * 3, axis=0))
        gain = lax.rsqrt(total * (1.0 / BANDW) + 1e-06)
        both = jnp.concatenate(
            [(re * gain).astype(jnp.bfloat16), (im * gain).astype(jnp.bfloat16)], axis=1
        )
        both = dot(both, order).astype(jnp.bfloat16)
        for q in range(quarters):
            part = both[q * chans : (q + 1) * chans]
            for n in range(max(1, 256 // width)):
                bins_ref[q * 256 // width + n, mine] = part[:, n * width : (n + 1) * width]
            for t in range(tm_count):
                rows_ref[t, w, :, q * 256 : (q + 1) * 256] = part[t * own : (t + 1) * own]
    for z in range(sizes["z"]):
        for y in range(sizes["y"]):
            bins_out[z][y] = bins_ref[chan_at(sizes, z, y)]
    for x in range(sizes["x"]):
        for c in range(sizes["c"]):
            rows_out[x * sizes["c"] + c][...] = rows_ref[tm_at(sizes, x, c)]


def whitened_spectra(strain, taps, sizes):
    chans, windows, samples = strain.shape
    rows = chans * windows
    chan_count = sizes["z"] * sizes["y"]
    tm_count = sizes["x"] * sizes["c"]
    width = SPEC // chan_count
    own = chans // tm_count
    x = jnp.transpose(strain, (1, 0, 2)).reshape(rows, samples)
    blocks = WIN // SUB
    filtered, _ = pl.pallas_call(
        functools.partial(fir_kernel, windows=windows),
        in_specs=[pl.BlockSpec(memory_space=pl.ANY)] * 2,
        out_specs=[pl.BlockSpec(memory_space=pltpu.VMEM)] * 2,
        out_shape=[
            jax.ShapeDtypeStruct((blocks, rows, 3 * SUB), jnp.bfloat16),
            jax.ShapeDtypeStruct((rows, samples), jnp.bfloat16),
        ],
        scratch_shapes=[
            pltpu.VMEM((1, TAPS), jnp.bfloat16),
            pltpu.VMEM((FIR_IN, FIR_OUT), jnp.bfloat16),
            pltpu.SemaphoreType.DMA((windows + 1,)),
        ],
        compiler_params=pltpu.CompilerParams(vmem_limit_bytes=58 * MIB),
        name="fir",
    )(x, taps.reshape(1, TAPS))
    part = dot(filtered.reshape(blocks * rows, 3 * SUB), jnp.asarray(forward_constants()))
    outs = pl.pallas_call(
        functools.partial(whiten_kernel, windows=windows, sizes=sizes),
        out_shape=[jax.ShapeDtypeStruct((sizes["y"], rows, width), jnp.bfloat16)] * sizes["z"]
        + [jax.ShapeDtypeStruct((windows, own, SPEC), jnp.bfloat16)] * tm_count,
        scratch_shapes=[
            pltpu.VMEM((chan_count, rows, width), jnp.bfloat16),
            pltpu.VMEM((tm_count, windows, own, SPEC), jnp.bfloat16),
        ],
        compiler_params=pltpu.CompilerParams(vmem_limit_bytes=24 * MIB),
        name="whiten",
    )(part.reshape(blocks, rows, SPEC))
    return outs[: sizes["z"]], outs[sizes["z"] :]


def pick_kernel(channels_ref, *refs, windows, sizes):
    bins = refs[: sizes["z"]]
    outs = refs[sizes["z"] :]
    chans = bins[0].shape[1] // windows
    sources = channels_ref.shape[1]
    chosen = []
    for z in range(sizes["z"]):
        first = chan_at(sizes, -z, 0) * chans
        ids = lax.broadcasted_iota(jnp.int32, (chans, sources), 0) + first
        chosen.append((ids == channels_ref[...]).astype(jnp.bfloat16))
    chosen = jnp.concatenate(chosen, axis=0)
    for y in range(sizes["y"]):
        for w in range(windows):
            block = jnp.concatenate([b[y, w * chans : (w + 1) * chans, :] for b in bins], axis=0)
            outs[y][0, w] = dot_tn(block, chosen).astype(jnp.bfloat16)


def picked_sources(source_channels, bins, windows, sizes):
    sources = source_channels.shape[0]
    width = bins[0].shape[2]
    shape = (1, windows, width, sources)
    parts = pl.pallas_call(
        functools.partial(pick_kernel, windows=windows, sizes=sizes),
        out_shape=[jax.ShapeDtypeStruct(shape, jnp.bfloat16)] * sizes["y"],
        compiler_params=pltpu.CompilerParams(vmem_limit_bytes=16 * MIB),
        name="pick",
    )(source_channels.reshape(1, sources), *bins)
    total = parts[0]
    for y in range(1, sizes["y"]):
        total = total + shifted(sizes, parts[y], y=y)
    return total


def block_at(sizes, step, sign):
    if sizes is None:
        return step
    z = lax.div(step, sizes["y"])
    y = lax.rem(step, sizes["y"])
    return chan_at(sizes, sign * z, sign * y)


def expand_kernel(*refs, sizes):
    out_ref = refs[-1]
    windows, own, _ = refs[0].shape
    depth = windows * (len(refs) - 1) * 2 * GROUP
    groups = 128 // (2 * GROUP)
    lane = lax.broadcasted_iota(jnp.int32, (own, 128), 1)
    first = lane % (2 * GROUP) < GROUP
    bin_row = lax.broadcasted_iota(jnp.int32, (own, GROUP, depth), 1)
    bin_lane = lax.broadcasted_iota(jnp.int32, (own, GROUP, depth), 2) % GROUP
    same = bin_row == bin_lane

    def body(step, carry):
        lanes = pl.ds(pl.multiple_of(block_at(sizes, step, -1) * 128, 128), 128)
        plain = []
        swapped = []
        for ref in refs[:-1]:
            for w in range(windows):
                x = ref[w, :, lanes].astype(jnp.float32)
                plain.append(x)
                ahead = pltpu.roll(x, 128 - GROUP, 1)
                behind = pltpu.roll(x, GROUP, 1)
                swapped.append(jnp.where(first, -ahead, behind))
        for g in range(groups):
            at = slice(g * 2 * GROUP, (g + 1) * 2 * GROUP)
            for p, parts in enumerate((plain, swapped)):
                a = jnp.concatenate([x[:, at] for x in parts], axis=1)
                full = jnp.where(same, a[:, None, :], 0.0)
                out_ref[step * groups + g, :, p * GROUP : (p + 1) * GROUP, :] = full.astype(jnp.bfloat16)
        return carry

    lax.fori_loop(0, SPEC // 128, body, 0)


def expanded_local(local, sizes):
    windows, own, _ = local[0].shape
    depth = windows * len(local) * 2 * GROUP
    out = pl.pallas_call(
        functools.partial(expand_kernel, sizes=sizes),
        out_shape=jax.ShapeDtypeStruct((SPEC // (2 * GROUP), own, 2 * GROUP, depth), jnp.bfloat16),
        cost_estimate=pl.CostEstimate(flops=4 * 10**9, bytes_accessed=8 * MIB, transcendentals=0),
        compiler_params=pltpu.CompilerParams(vmem_limit_bytes=24 * MIB),
        name="expand",
    )(*local)
    return out.reshape(SPEC // (2 * GROUP), own * 2 * GROUP, depth)


def cross_kernel(local_ref, *refs, fetch, own, sizes, by_y):
    sources = refs[:-1]
    out_ref = refs[-1]
    count = sources[0].shape[-1]
    groups = 128 // (2 * GROUP)
    row = lax.broadcasted_iota(jnp.int32, (count, count), 0)
    column = lax.broadcasted_iota(jnp.int32, (count, count), 1)
    identity = (row == column).astype(jnp.bfloat16)

    def body(index, carry):
        step = index if by_y is None else index * sizes["y"] + by_y
        tiles = fetch(sources, step)
        cross = []
        for g in range(groups):
            rows = slice(g * 2 * GROUP, (g + 1) * 2 * GROUP)
            block = jnp.concatenate([tile[rows] for tile in tiles], axis=0)
            cross.append(dot(local_ref[step * groups + g], block).astype(jnp.bfloat16))
        tall = jnp.concatenate(
            [x[c * 2 * GROUP : (c + 1) * 2 * GROUP] for c in range(own) for x in cross], axis=0
        )
        turned = dot_nt(identity, tall)
        by_channel = jnp.stack([turned[:, c * 128 : (c + 1) * 128] for c in range(own)], axis=0)
        mixed = jnp.transpose(by_channel, (1, 0, 2)).reshape(count * own, 128)
        block = step if sizes is None else lax.div(block_at(sizes, step, -1), sizes["y"])
        out_ref[:, pl.ds(pl.multiple_of(block * 128, 128), 128)] = mixed.astype(jnp.bfloat16)
        return carry

    lax.fori_loop(0, SPEC // 128 if by_y is None else sizes["z"], body, 0)


def crossed(local, sources, fetch, sizes, by_y=None):
    _, expanded_rows, _ = local.shape
    own = expanded_rows // (2 * GROUP)
    count = sources[0].shape[-1]
    columns = SPEC if by_y is None else 128 * sizes["z"]
    return pl.pallas_call(
        functools.partial(cross_kernel, fetch=fetch, own=own, sizes=sizes, by_y=by_y),
        out_shape=jax.ShapeDtypeStruct((count * own, columns), jnp.bfloat16),
        cost_estimate=pl.CostEstimate(flops=4 * 10**9, bytes_accessed=8 * MIB, transcendentals=0),
        compiler_params=pltpu.CompilerParams(vmem_limit_bytes=32 * MIB),
        name="cross",
    )(local, *sources)


def table_rows(table_ref, columns, sizes, by_y):
    if by_y is None:
        return table_ref[...]
    y = lax.rem(chan_at(sizes, 0, -by_y), sizes["y"])
    rows = [pl.ds(pl.multiple_of((z * sizes["y"] + y) * 128, 128), 128) for z in range(columns // 128)]
    return jnp.concatenate([table_ref[r] for r in rows], axis=0)


def part_kernel(cross_ref, table_ref, out_ref, chosen, *, sizes, by_y):
    chosen[...] = table_rows(table_ref, cross_ref.shape[1], sizes, by_y)
    height = 512

    def body(i, carry):
        mine = pl.ds(pl.multiple_of(i * height, height), height)
        rows = cross_ref[mine]
        for n in range(LAGS // 256):
            at = slice(n * 256, (n + 1) * 256)
            out_ref[mine, at] = dot(rows, chosen[:, at])
        return carry

    lax.fori_loop(0, cross_ref.shape[0] // height, body, 0)


def lag_kernel(*refs, scale, sizes, by_y):
    cross_ref, table_ref = refs[:2]
    chosen, buffer, sems = refs[-3:]
    out_hbm = refs[-4]
    earlier = refs[2:-4]
    depth, height, lags = buffer.shape
    steps = cross_ref.shape[0] // height
    chosen[...] = table_rows(table_ref, cross_ref.shape[1], sizes, by_y)

    def store(i):
        mine = pl.ds(pl.multiple_of(i * height, height), height)
        slot = lax.rem(i, depth)
        return pltpu.make_async_copy(buffer.at[slot], out_hbm.at[mine], sems.at[slot])

    def body(i, carry):
        @pl.when(i >= depth)
        def _():
            store(i - depth).wait()

        mine = pl.ds(pl.multiple_of(i * height, height), height)
        rows = cross_ref[mine]
        slot = lax.rem(i, depth)
        for n in range(lags // 256):
            at = slice(n * 256, (n + 1) * 256)
            total = dot(rows, chosen[:, at])
            for held in earlier:
                total = total + held[mine, at]
            buffer[slot, :, at] = total * scale
        store(i).start()
        return carry

    lax.fori_loop(0, steps, body, 0)
    for i in range(max(0, steps - depth), steps):
        store(i).wait()


def lag_parts(cross, sizes, by_y):
    rows, columns = cross.shape
    return pl.pallas_call(
        functools.partial(part_kernel, sizes=sizes, by_y=by_y),
        out_shape=jax.ShapeDtypeStruct((rows, LAGS), jnp.float32),
        scratch_shapes=[pltpu.VMEM((columns, LAGS), jnp.bfloat16)],
        cost_estimate=pl.CostEstimate(flops=4 * 10**9, bytes_accessed=8 * MIB, transcendentals=0),
        compiler_params=pltpu.CompilerParams(vmem_limit_bytes=24 * MIB),
        name="lags_near",
    )(cross, jnp.asarray(lag_constant()))


def correlations(cross, earlier, window_total, sizes=None, by_y=None):
    rows, columns = cross.shape
    height = 256
    return pl.pallas_call(
        functools.partial(
            lag_kernel, scale=1.0 / math.sqrt(NFREQ * window_total), sizes=sizes, by_y=by_y
        ),
        in_specs=[pl.BlockSpec(memory_space=pltpu.VMEM)] * (2 + len(earlier)),
        out_specs=pl.BlockSpec(memory_space=pl.ANY),
        out_shape=jax.ShapeDtypeStruct((rows, LAGS), jnp.float32),
        scratch_shapes=[
            pltpu.VMEM((columns, LAGS), jnp.bfloat16),
            pltpu.VMEM((3, height, LAGS), jnp.float32),
            pltpu.SemaphoreType.DMA((3,)),
        ],
        compiler_params=pltpu.CompilerParams(vmem_limit_bytes=24 * MIB),
        name="lags",
    )(cross, jnp.asarray(lag_constant()), *earlier)


def gathered(picked, local, window_total, sizes):
    windows, width = picked.shape[1:3]
    half = width // 2
    whole = jnp.concatenate([shifted(sizes, picked, z=d) for d in range(sizes["z"])], axis=0)
    held = {(0, 0): [whole]}
    for x in range(1, sizes["x"]):
        held[x, 0] = [shifted(sizes, whole, x=x)]
    for y in range(1, sizes["y"]):
        held[0, y] = [shifted(sizes, whole, y=y)]
    expanded = expanded_local(local, sizes)
    edges = {key: array for key, array in held.items() if key != (0, 0)}
    edges, expanded = lax.optimization_barrier((edges, expanded))
    held.update(edges)
    for x in range(1, sizes["x"]):
        for y in range(1, sizes["y"]):
            held[x, y] = [
                shifted(sizes, held[0, y][0][:, :, :half], x=x),
                shifted(sizes, held[x, 0][0][:, :, half:], y=y),
            ]

    def rows_of(y):
        arrays = []
        place = {}
        for x in range(sizes["x"]):
            for c in range(sizes["c"]):
                place[x, c] = len(arrays)
                arrays += [shifted(sizes, array, c=c) for array in held[x, y]]

        def fetch(refs, step):
            by_z = lax.div(step, sizes["y"])
            tiles = []
            for x in range(sizes["x"]):
                for c in range(sizes["c"]):
                    parts = refs[place[x, c] : place[x, c] + len(held[x, y])]
                    for w in range(windows):
                        tiles.append(jnp.concatenate([part[by_z, w] for part in parts], axis=0))
            return tiles

        return arrays, fetch

    earlier = []
    for y in range(sizes["y"]):
        if y > 0:
            far = {key: array for key, array in held.items() if key[0] and key[1]}
            far, cross = lax.optimization_barrier((far, cross))
            held.update(far)
            earlier.append(lag_parts(cross, sizes, y - 1))
        arrays, fetch = rows_of(y)
        cross = crossed(expanded, arrays, fetch, sizes, by_y=y)
    return correlations(cross, earlier, window_total, sizes, sizes["y"] - 1)


def gathered_plainly(picked, local, window_total, sizes):
    parts = [shifted(sizes, picked, x=x, c=c) for x in range(sizes["x"]) for c in range(sizes["c"])]
    mine = jnp.concatenate(parts, axis=1)[0]
    total, width, count = mine.shape
    held = lax.all_gather(mine, "chan", axis=0, tiled=False)
    held = held.reshape(SPEC // 128, 128 // width, total, width, count)
    held = jnp.transpose(held, (0, 2, 1, 3, 4)).reshape(SPEC // 128, total, 128, count)

    def fetch(refs, step):
        return [refs[0][step, i] for i in range(total)]

    cross = crossed(expanded_local(local, None), [held], fetch, None)
    return correlations(cross, [], window_total)


def on_device(strain_rate, fir_taps, source_channels):
    sizes = factors(lax.axis_size("chan"), lax.axis_size("tm"))
    windows = strain_rate.shape[1]
    bins, rows = whitened_spectra(strain_rate, fir_taps, sizes)
    bins = [shifted(sizes, b, z=z) for z, b in enumerate(bins)]
    moves = [(x, c) for x in range(sizes["x"]) for c in range(sizes["c"])]
    local = [shifted(sizes, r, x=x, c=c) for r, (x, c) in zip(rows, moves)]
    bins, local = lax.optimization_barrier((bins, local))
    picked = picked_sources(source_channels, bins, windows, sizes)
    gather = gathered if picked.shape[2] == 128 else gathered_plainly
    out = gather(picked, local, windows * lax.axis_size("tm"), sizes)
    return out.reshape(source_channels.shape[0], -1, LAGS)


def solution(mesh):
    placed = (P("chan", "tm", None), P(), P())
    return jax.shard_map(
        on_device,
        mesh=mesh,
        in_specs=placed,
        out_specs=P(None, ("chan", "tm"), None),
        check_vma=False,
    )
```

```python
import functools
import math

import jax
import jax.numpy as jnp
import numpy as np
from jax import lax
from jax.experimental import pallas as pl
from jax.experimental.pallas import tpu as pltpu
from jax.sharding import PartitionSpec as P

WIN = 4096
NFREQ = 512
BANDW = 64
K_LO = 32
LAGS = 1024
TAPS = 32
SUB = 512
GROUP = 8
SPEC = 2 * NFREQ
FIR_OUT = 256
FIR_IN = 4 * FIR_OUT + 128
MIB = 1 << 20


def forward_constants():
    samples = np.arange(SUB)[:, None]
    bins = np.arange(NFREQ)[None, :] + K_LO
    angles = 2.0 * np.pi * ((samples * bins) % (2 * WIN)) / (2 * WIN)
    table = np.concatenate([np.cos(angles), -np.sin(angles)], axis=1)
    high = table.astype(jnp.bfloat16)
    low = (table - high.astype(np.float64)).astype(jnp.bfloat16)
    return np.concatenate([high, high, low], axis=0)


def lag_constant():
    group, part, inner = np.meshgrid(
        np.arange(NFREQ // GROUP), np.arange(2), np.arange(GROUP), indexing="ij"
    )
    bins = (group * GROUP + inner).reshape(-1, 1) + K_LO
    lags = np.arange(LAGS)[None, :] - LAGS // 2 + 2 * WIN
    angles = 2.0 * np.pi * ((bins * lags) % (2 * WIN)) / (2 * WIN)
    table = np.where(part.reshape(-1, 1) == 0, np.cos(angles), -np.sin(angles))
    return table.astype(jnp.bfloat16)


def dot(a, b):
    return jnp.dot(a, b, preferred_element_type=jnp.float32)


def dot_nt(a, b):
    return lax.dot_general(a, b, (((1,), (1,)), ((), ())), preferred_element_type=jnp.float32)


def dot_tn(a, b):
    return lax.dot_general(a, b, (((0,), (0,)), ((), ())), preferred_element_type=jnp.float32)


def split(x):
    high = x.astype(jnp.bfloat16)
    return high, (x - high.astype(jnp.float32)).astype(jnp.bfloat16)


def turn_values(shape):
    index = (lax.broadcasted_iota(jnp.int32, shape, 1) + K_LO) % 16
    real = jnp.zeros(shape, jnp.float32)
    imag = jnp.zeros(shape, jnp.float32)
    for i in range(16):
        real = jnp.where(index == i, math.cos(math.pi * i / 8), real)
        imag = jnp.where(index == i, -math.sin(math.pi * i / 8), imag)
    return real, imag


def factors(chan_count, tm_count):
    inner = 2 if chan_count <= 8 else 4
    return {"z": chan_count // inner, "y": inner, "x": tm_count // 2, "c": 2}


def moved(sizes, index, outer, inner, by_outer, by_inner):
    n_outer, n_inner = sizes[outer], sizes[inner]
    hi = lax.rem(lax.div(index, n_inner) + by_outer + n_outer, n_outer)
    lo = lax.rem(lax.rem(index, n_inner) + by_inner + n_inner, n_inner)
    return hi * n_inner + lo


def chan_at(sizes, by_z, by_y):
    return moved(sizes, lax.axis_index("chan"), "z", "y", by_z, by_y)


def tm_at(sizes, by_x, by_c):
    return moved(sizes, lax.axis_index("tm"), "x", "c", by_x, by_c)


def shifted(sizes, value, **by):
    if not any(by.values()):
        return value
    axis, outer, inner = ("chan", "z", "y") if set(by) <= {"z", "y"} else ("tm", "x", "c")
    n_outer, n_inner = sizes[outer], sizes[inner]
    pairs = []
    for index in range(n_outer * n_inner):
        hi = (index // n_inner + by.get(outer, 0)) % n_outer
        lo = (index % n_inner + by.get(inner, 0)) % n_inner
        pairs.append((index, hi * n_inner + lo))
    return lax.ppermute(value, axis, pairs)


def filter_matrix(taps, toeplitz):
    in_index = lax.broadcasted_iota(jnp.int32, (256, 128), 0)
    out_index = lax.broadcasted_iota(jnp.int32, (256, 128), 1)
    tap = in_index - 4 * (out_index % TAPS) - 97
    small = jnp.zeros((256, 128), jnp.float32)
    for j in range(TAPS):
        small = jnp.where(tap == j, taps[0:1, j : j + 1], small)
    slot = lax.broadcasted_iota(jnp.int32, (128, 128), 1) // TAPS
    for a in range(FIR_IN // 128):
        for n in range(FIR_OUT // 128):
            here = jnp.where(slot + n * (128 // TAPS) == a, small[:128], 0.0)
            here = jnp.where(slot + n * (128 // TAPS) == a - 1, small[128:], here)
            toeplitz[a * 128 : (a + 1) * 128, n * 128 : (n + 1) * 128] = here.astype(jnp.bfloat16)


def fir_kernel(x_hbm, fir_hbm, out_ref, x_ref, fir_ref, toeplitz, sems, *, windows):
    chans = x_ref.shape[0] // windows
    fetch_fir = pltpu.make_async_copy(fir_hbm, fir_ref, sems.at[windows])
    fetch_fir.start()
    fetches = []
    for w in range(windows):
        mine = pl.ds(w * chans, chans)
        fetches.append(pltpu.make_async_copy(x_hbm.at[mine], x_ref.at[mine], sems.at[w]))
        fetches[-1].start()
    fetch_fir.wait()
    filter_matrix(fir_ref[...].astype(jnp.float32), toeplitz)
    step = 4 * FIR_OUT
    per = SUB // FIR_OUT
    together = 4

    def work(pieces, mine, first):
        piece = dot(jnp.concatenate(pieces, axis=0), toeplitz[...])
        high, low = split(piece)
        for n in range(together):
            i = (first + n) // per
            at = (n % per) * FIR_OUT
            part = slice(n * chans, (n + 1) * chans)
            out_ref[i, mine, at : at + FIR_OUT] = high[part]
            out_ref[i, mine, SUB + at : SUB + at + FIR_OUT] = low[part]
            out_ref[i, mine, 2 * SUB + at : 2 * SUB + at + FIR_OUT] = high[part]

    for w in range(windows):
        mine = slice(w * chans, (w + 1) * chans)
        fetches[w].wait()
        pieces = [jnp.concatenate([jnp.zeros((chans, 128), jnp.bfloat16), x_ref[mine, :step]], axis=1)]
        for n in range(1, together):
            pieces.append(x_ref[mine, n * step - 128 : (n + 1) * step])
        work(pieces, mine, 0)

        def body(j, carry, mine=mine):
            pieces = []
            for n in range(together):
                first = pl.multiple_of((j * together + n) * step - 128, 128)
                pieces.append(x_ref[mine, pl.ds(first, step + 128)])
            work(pieces, mine, j * together)
            return carry

        lax.fori_loop(1, WIN // FIR_OUT // together, body, 0)


def whiten_kernel(part_ref, *refs, windows, sizes):
    tm_count = sizes["x"] * sizes["c"]
    bins_out = refs[: sizes["z"]]
    rows_out = refs[sizes["z"] : sizes["z"] + tm_count]
    bins_ref, rows_ref = refs[sizes["z"] + tm_count :]
    blocks, rows, _ = part_ref.shape
    chans = rows // windows
    width = bins_ref.shape[2]
    own = rows_ref.shape[2]
    quarters = NFREQ // 128
    turn_re, turn_im = turn_values((1, NFREQ))
    band_a = lax.broadcasted_iota(jnp.int32, (128, 128), 0) // BANDW
    band_b = lax.broadcasted_iota(jnp.int32, (128, 128), 1) // BANDW
    same_band = (band_a == band_b).astype(jnp.bfloat16)
    src = lax.broadcasted_iota(jnp.int32, (256, 256), 0)
    dst = lax.broadcasted_iota(jnp.int32, (256, 256), 1)
    wanted = (dst // (2 * GROUP)) * GROUP + dst % GROUP + 128 * ((dst // GROUP) % 2)
    order = (src == wanted).astype(jnp.bfloat16)
    for w in range(windows):
        mine = slice(w * chans, (w + 1) * chans)
        real = part_ref[blocks - 1, mine, :NFREQ]
        imag = part_ref[blocks - 1, mine, NFREQ:]
        for i in reversed(range(blocks - 1)):
            real, imag = (
                part_ref[i, mine, :NFREQ] + real * turn_re - imag * turn_im,
                part_ref[i, mine, NFREQ:] + real * turn_im + imag * turn_re,
            )
        re = jnp.concatenate([real[:, q * 128 : (q + 1) * 128] for q in range(quarters)], axis=0)
        im = jnp.concatenate([imag[:, q * 128 : (q + 1) * 128] for q in range(quarters)], axis=0)
        power = re * re + im * im
        p0, p1 = split(power)
        p2 = (power - p0.astype(jnp.float32) - p1.astype(jnp.float32)).astype(jnp.bfloat16)
        total = dot(jnp.concatenate([p0, p1, p2], axis=1), jnp.concatenate([same_band] * 3, axis=0))
        gain = lax.rsqrt(total * (1.0 / BANDW) + 1e-06)
        both = jnp.concatenate(
            [(re * gain).astype(jnp.bfloat16), (im * gain).astype(jnp.bfloat16)], axis=1
        )
        both = dot(both, order).astype(jnp.bfloat16)
        for q in range(quarters):
            part = both[q * chans : (q + 1) * chans]
            for n in range(max(1, 256 // width)):
                bins_ref[q * 256 // width + n, mine] = part[:, n * width : (n + 1) * width]
            for t in range(tm_count):
                rows_ref[t, w, :, q * 256 : (q + 1) * 256] = part[t * own : (t + 1) * own]
    for z in range(sizes["z"]):
        for y in range(sizes["y"]):
            bins_out[z][y] = bins_ref[chan_at(sizes, z, y)]
    for x in range(sizes["x"]):
        for c in range(sizes["c"]):
            rows_out[x * sizes["c"] + c][...] = rows_ref[tm_at(sizes, x, c)]


def whitened_spectra(strain, taps, sizes):
    chans, windows, samples = strain.shape
    rows = chans * windows
    chan_count = sizes["z"] * sizes["y"]
    tm_count = sizes["x"] * sizes["c"]
    width = SPEC // chan_count
    own = chans // tm_count
    x = jnp.transpose(strain, (1, 0, 2)).reshape(rows, samples)
    blocks = WIN // SUB
    filtered = pl.pallas_call(
        functools.partial(fir_kernel, windows=windows),
        in_specs=[pl.BlockSpec(memory_space=pl.ANY)] * 2,
        out_shape=jax.ShapeDtypeStruct((blocks, rows, 3 * SUB), jnp.bfloat16),
        scratch_shapes=[
            pltpu.VMEM((rows, samples), jnp.bfloat16),
            pltpu.VMEM((1, TAPS), jnp.bfloat16),
            pltpu.VMEM((FIR_IN, FIR_OUT), jnp.bfloat16),
            pltpu.SemaphoreType.DMA((windows + 1,)),
        ],
        compiler_params=pltpu.CompilerParams(vmem_limit_bytes=46 * MIB),
        name="fir",
    )(x, taps.reshape(1, TAPS))
    part = dot(filtered.reshape(blocks * rows, 3 * SUB), jnp.asarray(forward_constants()))
    outs = pl.pallas_call(
        functools.partial(whiten_kernel, windows=windows, sizes=sizes),
        out_shape=[jax.ShapeDtypeStruct((sizes["y"], rows, width), jnp.bfloat16)] * sizes["z"]
        + [jax.ShapeDtypeStruct((windows, own, SPEC), jnp.bfloat16)] * tm_count,
        scratch_shapes=[
            pltpu.VMEM((chan_count, rows, width), jnp.bfloat16),
            pltpu.VMEM((tm_count, windows, own, SPEC), jnp.bfloat16),
        ],
        compiler_params=pltpu.CompilerParams(vmem_limit_bytes=24 * MIB),
        name="whiten",
    )(part.reshape(blocks, rows, SPEC))
    return outs[: sizes["z"]], outs[sizes["z"] :]


def pick_kernel(channels_ref, *refs, windows, sizes):
    bins = refs[: sizes["z"]]
    outs = refs[sizes["z"] :]
    chans = bins[0].shape[1] // windows
    sources = channels_ref.shape[1]
    chosen = []
    for z in range(sizes["z"]):
        first = chan_at(sizes, -z, 0) * chans
        ids = lax.broadcasted_iota(jnp.int32, (chans, sources), 0) + first
        chosen.append((ids == channels_ref[...]).astype(jnp.bfloat16))
    chosen = jnp.concatenate(chosen, axis=0)
    for y in range(sizes["y"]):
        for w in range(windows):
            block = jnp.concatenate([b[y, w * chans : (w + 1) * chans, :] for b in bins], axis=0)
            outs[y][0, w] = dot_tn(block, chosen).astype(jnp.bfloat16)


def picked_sources(source_channels, bins, windows, sizes):
    sources = source_channels.shape[0]
    width = bins[0].shape[2]
    shape = (1, windows, width, sources)
    parts = pl.pallas_call(
        functools.partial(pick_kernel, windows=windows, sizes=sizes),
        out_shape=[jax.ShapeDtypeStruct(shape, jnp.bfloat16)] * sizes["y"],
        compiler_params=pltpu.CompilerParams(vmem_limit_bytes=16 * MIB),
        name="pick",
    )(source_channels.reshape(1, sources), *bins)
    total = parts[0]
    for y in range(1, sizes["y"]):
        total = total + shifted(sizes, parts[y], y=y)
    return total


def block_at(sizes, step, sign):
    if sizes is None:
        return step
    z = lax.div(step, sizes["y"])
    y = lax.rem(step, sizes["y"])
    return chan_at(sizes, sign * z, sign * y)


def expand_kernel(*refs, sizes):
    out_ref = refs[-1]
    windows, own, _ = refs[0].shape
    depth = windows * (len(refs) - 1) * 2 * GROUP
    groups = 128 // (2 * GROUP)
    lane = lax.broadcasted_iota(jnp.int32, (own, 128), 1)
    first = lane % (2 * GROUP) < GROUP
    bin_row = lax.broadcasted_iota(jnp.int32, (own, GROUP, depth), 1)
    bin_lane = lax.broadcasted_iota(jnp.int32, (own, GROUP, depth), 2) % GROUP
    same = bin_row == bin_lane

    def body(step, carry):
        lanes = pl.ds(pl.multiple_of(block_at(sizes, step, -1) * 128, 128), 128)
        plain = []
        swapped = []
        for ref in refs[:-1]:
            for w in range(windows):
                x = ref[w, :, lanes].astype(jnp.float32)
                plain.append(x)
                ahead = pltpu.roll(x, 128 - GROUP, 1)
                behind = pltpu.roll(x, GROUP, 1)
                swapped.append(jnp.where(first, -ahead, behind))
        for g in range(groups):
            at = slice(g * 2 * GROUP, (g + 1) * 2 * GROUP)
            for p, parts in enumerate((plain, swapped)):
                a = jnp.concatenate([x[:, at] for x in parts], axis=1)
                full = jnp.where(same, a[:, None, :], 0.0)
                out_ref[step * groups + g, :, p * GROUP : (p + 1) * GROUP, :] = full.astype(jnp.bfloat16)
        return carry

    lax.fori_loop(0, SPEC // 128, body, 0)


def expanded_local(local, sizes):
    windows, own, _ = local[0].shape
    depth = windows * len(local) * 2 * GROUP
    out = pl.pallas_call(
        functools.partial(expand_kernel, sizes=sizes),
        out_shape=jax.ShapeDtypeStruct((SPEC // (2 * GROUP), own, 2 * GROUP, depth), jnp.bfloat16),
        cost_estimate=pl.CostEstimate(flops=4 * 10**9, bytes_accessed=8 * MIB, transcendentals=0),
        compiler_params=pltpu.CompilerParams(vmem_limit_bytes=24 * MIB),
        name="expand",
    )(*local)
    return out.reshape(SPEC // (2 * GROUP), own * 2 * GROUP, depth)


def cross_kernel(local_ref, *refs, fetch, own, sizes, by_y):
    sources = refs[:-1]
    out_ref = refs[-1]
    count = sources[0].shape[-1]
    groups = 128 // (2 * GROUP)
    row = lax.broadcasted_iota(jnp.int32, (count, count), 0)
    column = lax.broadcasted_iota(jnp.int32, (count, count), 1)
    identity = (row == column).astype(jnp.bfloat16)

    def body(index, carry):
        step = index if by_y is None else index * sizes["y"] + by_y
        tiles = fetch(sources, step)
        cross = []
        for g in range(groups):
            rows = slice(g * 2 * GROUP, (g + 1) * 2 * GROUP)
            block = jnp.concatenate([tile[rows] for tile in tiles], axis=0)
            cross.append(dot(local_ref[step * groups + g], block).astype(jnp.bfloat16))
        tall = jnp.concatenate(
            [x[c * 2 * GROUP : (c + 1) * 2 * GROUP] for c in range(own) for x in cross], axis=0
        )
        turned = dot_nt(identity, tall)
        by_channel = jnp.stack([turned[:, c * 128 : (c + 1) * 128] for c in range(own)], axis=0)
        mixed = jnp.transpose(by_channel, (1, 0, 2)).reshape(count * own, 128)
        block = step if sizes is None else lax.div(block_at(sizes, step, -1), sizes["y"])
        out_ref[:, pl.ds(pl.multiple_of(block * 128, 128), 128)] = mixed.astype(jnp.bfloat16)
        return carry

    lax.fori_loop(0, SPEC // 128 if by_y is None else sizes["z"], body, 0)


def crossed(local, sources, fetch, sizes, by_y=None):
    _, expanded_rows, _ = local.shape
    own = expanded_rows // (2 * GROUP)
    count = sources[0].shape[-1]
    columns = SPEC if by_y is None else 128 * sizes["z"]
    return pl.pallas_call(
        functools.partial(cross_kernel, fetch=fetch, own=own, sizes=sizes, by_y=by_y),
        out_shape=jax.ShapeDtypeStruct((count * own, columns), jnp.bfloat16),
        cost_estimate=pl.CostEstimate(flops=4 * 10**9, bytes_accessed=8 * MIB, transcendentals=0),
        compiler_params=pltpu.CompilerParams(vmem_limit_bytes=32 * MIB),
        name="cross",
    )(local, *sources)


def table_rows(table_ref, columns, sizes, by_y):
    if by_y is None:
        return table_ref[...]
    y = lax.rem(chan_at(sizes, 0, -by_y), sizes["y"])
    rows = [pl.ds(pl.multiple_of((z * sizes["y"] + y) * 128, 128), 128) for z in range(columns // 128)]
    return jnp.concatenate([table_ref[r] for r in rows], axis=0)


def part_kernel(cross_ref, table_ref, out_ref, chosen, *, sizes, by_y):
    chosen[...] = table_rows(table_ref, cross_ref.shape[1], sizes, by_y)
    height = 512

    def body(i, carry):
        mine = pl.ds(pl.multiple_of(i * height, height), height)
        rows = cross_ref[mine]
        for n in range(LAGS // 256):
            at = slice(n * 256, (n + 1) * 256)
            out_ref[mine, at] = dot(rows, chosen[:, at])
        return carry

    lax.fori_loop(0, cross_ref.shape[0] // height, body, 0)


def lag_kernel(*refs, scale, sizes, by_y):
    cross_ref, table_ref = refs[:2]
    chosen, buffer, sems = refs[-3:]
    out_hbm = refs[-4]
    earlier = refs[2:-4]
    depth, height, lags = buffer.shape
    steps = cross_ref.shape[0] // height
    chosen[...] = table_rows(table_ref, cross_ref.shape[1], sizes, by_y)

    def store(i):
        mine = pl.ds(pl.multiple_of(i * height, height), height)
        slot = lax.rem(i, depth)
        return pltpu.make_async_copy(buffer.at[slot], out_hbm.at[mine], sems.at[slot])

    def body(i, carry):
        @pl.when(i >= depth)
        def _():
            store(i - depth).wait()

        mine = pl.ds(pl.multiple_of(i * height, height), height)
        rows = cross_ref[mine]
        slot = lax.rem(i, depth)
        for n in range(lags // 256):
            at = slice(n * 256, (n + 1) * 256)
            total = dot(rows, chosen[:, at])
            for held in earlier:
                total = total + held[mine, at]
            buffer[slot, :, at] = total * scale
        store(i).start()
        return carry

    lax.fori_loop(0, steps, body, 0)
    for i in range(max(0, steps - depth), steps):
        store(i).wait()


def lag_parts(cross, sizes, by_y):
    rows, columns = cross.shape
    return pl.pallas_call(
        functools.partial(part_kernel, sizes=sizes, by_y=by_y),
        out_shape=jax.ShapeDtypeStruct((rows, LAGS), jnp.float32),
        scratch_shapes=[pltpu.VMEM((columns, LAGS), jnp.bfloat16)],
        cost_estimate=pl.CostEstimate(flops=4 * 10**9, bytes_accessed=8 * MIB, transcendentals=0),
        compiler_params=pltpu.CompilerParams(vmem_limit_bytes=24 * MIB),
        name="lags_near",
    )(cross, jnp.asarray(lag_constant()))


def correlations(cross, earlier, window_total, sizes=None, by_y=None):
    rows, columns = cross.shape
    height = 256
    return pl.pallas_call(
        functools.partial(
            lag_kernel, scale=1.0 / math.sqrt(NFREQ * window_total), sizes=sizes, by_y=by_y
        ),
        in_specs=[pl.BlockSpec(memory_space=pltpu.VMEM)] * (2 + len(earlier)),
        out_specs=pl.BlockSpec(memory_space=pl.ANY),
        out_shape=jax.ShapeDtypeStruct((rows, LAGS), jnp.float32),
        scratch_shapes=[
            pltpu.VMEM((columns, LAGS), jnp.bfloat16),
            pltpu.VMEM((3, height, LAGS), jnp.float32),
            pltpu.SemaphoreType.DMA((3,)),
        ],
        compiler_params=pltpu.CompilerParams(vmem_limit_bytes=24 * MIB),
        name="lags",
    )(cross, jnp.asarray(lag_constant()), *earlier)


def gathered(picked, local, window_total, sizes):
    windows, width = picked.shape[1:3]
    half = width // 2
    whole = jnp.concatenate([shifted(sizes, picked, z=d) for d in range(sizes["z"])], axis=0)
    held = {(0, 0): [whole]}
    for x in range(1, sizes["x"]):
        held[x, 0] = [shifted(sizes, whole, x=x)]
    for y in range(1, sizes["y"]):
        held[0, y] = [shifted(sizes, whole, y=y)]
    expanded = expanded_local(local, sizes)
    edges = {key: array for key, array in held.items() if key != (0, 0)}
    edges, expanded = lax.optimization_barrier((edges, expanded))
    held.update(edges)
    for x in range(1, sizes["x"]):
        for y in range(1, sizes["y"]):
            held[x, y] = [
                shifted(sizes, held[0, y][0][:, :, :half], x=x),
                shifted(sizes, held[x, 0][0][:, :, half:], y=y),
            ]

    def rows_of(y):
        arrays = []
        place = {}
        for x in range(sizes["x"]):
            for c in range(sizes["c"]):
                place[x, c] = len(arrays)
                arrays += [shifted(sizes, array, c=c) for array in held[x, y]]

        def fetch(refs, step):
            by_z = lax.div(step, sizes["y"])
            tiles = []
            for x in range(sizes["x"]):
                for c in range(sizes["c"]):
                    parts = refs[place[x, c] : place[x, c] + len(held[x, y])]
                    for w in range(windows):
                        tiles.append(jnp.concatenate([part[by_z, w] for part in parts], axis=0))
            return tiles

        return arrays, fetch

    earlier = []
    for y in range(sizes["y"]):
        if y > 0:
            far = {key: array for key, array in held.items() if key[0] and key[1]}
            far, cross = lax.optimization_barrier((far, cross))
            held.update(far)
            earlier.append(lag_parts(cross, sizes, y - 1))
        arrays, fetch = rows_of(y)
        cross = crossed(expanded, arrays, fetch, sizes, by_y=y)
    return correlations(cross, earlier, window_total, sizes, sizes["y"] - 1)


def gathered_plainly(picked, local, window_total, sizes):
    parts = [shifted(sizes, picked, x=x, c=c) for x in range(sizes["x"]) for c in range(sizes["c"])]
    mine = jnp.concatenate(parts, axis=1)[0]
    total, width, count = mine.shape
    held = lax.all_gather(mine, "chan", axis=0, tiled=False)
    held = held.reshape(SPEC // 128, 128 // width, total, width, count)
    held = jnp.transpose(held, (0, 2, 1, 3, 4)).reshape(SPEC // 128, total, 128, count)

    def fetch(refs, step):
        return [refs[0][step, i] for i in range(total)]

    cross = crossed(expanded_local(local, None), [held], fetch, None)
    return correlations(cross, [], window_total)


def on_device(strain_rate, fir_taps, source_channels):
    sizes = factors(lax.axis_size("chan"), lax.axis_size("tm"))
    windows = strain_rate.shape[1]
    bins, rows = whitened_spectra(strain_rate, fir_taps, sizes)
    bins = [shifted(sizes, b, z=z) for z, b in enumerate(bins)]
    moves = [(x, c) for x in range(sizes["x"]) for c in range(sizes["c"])]
    local = [shifted(sizes, r, x=x, c=c) for r, (x, c) in zip(rows, moves)]
    bins, local = lax.optimization_barrier((bins, local))
    picked = picked_sources(source_channels, bins, windows, sizes)
    gather = gathered if picked.shape[2] == 128 else gathered_plainly
    out = gather(picked, local, windows * lax.axis_size("tm"), sizes)
    return out.reshape(source_channels.shape[0], -1, LAGS)


def solution(mesh):
    placed = (P("chan", "tm", None), P(), P())
    return jax.shard_map(
        on_device,
        mesh=mesh,
        in_specs=placed,
        out_specs=P(None, ("chan", "tm"), None),
        check_vma=False,
    )
```

```python
import functools
import math

import jax
import jax.numpy as jnp
import numpy as np
from jax import lax
from jax.experimental import pallas as pl
from jax.experimental.pallas import tpu as pltpu
from jax.sharding import PartitionSpec as P

WIN = 4096
NFREQ = 512
BANDW = 64
K_LO = 32
LAGS = 1024
TAPS = 32
SUB = 512
GROUP = 8
SPEC = 2 * NFREQ
FIR_OUT = 256
FIR_IN = 4 * FIR_OUT + 128
MIB = 1 << 20


def forward_constants():
    samples = np.arange(SUB)[:, None]
    bins = np.arange(NFREQ)[None, :] + K_LO
    angles = 2.0 * np.pi * ((samples * bins) % (2 * WIN)) / (2 * WIN)
    table = np.concatenate([np.cos(angles), -np.sin(angles)], axis=1)
    high = table.astype(jnp.bfloat16)
    low = (table - high.astype(np.float64)).astype(jnp.bfloat16)
    return np.concatenate([high, high, low], axis=0)


def lag_constant():
    group, part, inner = np.meshgrid(
        np.arange(NFREQ // GROUP), np.arange(2), np.arange(GROUP), indexing="ij"
    )
    bins = (group * GROUP + inner).reshape(-1, 1) + K_LO
    lags = np.arange(LAGS)[None, :] - LAGS // 2 + 2 * WIN
    angles = 2.0 * np.pi * ((bins * lags) % (2 * WIN)) / (2 * WIN)
    table = np.where(part.reshape(-1, 1) == 0, np.cos(angles), -np.sin(angles))
    return table.astype(jnp.bfloat16)


def dot(a, b):
    return jnp.dot(a, b, preferred_element_type=jnp.float32)


def dot_nt(a, b):
    return lax.dot_general(a, b, (((1,), (1,)), ((), ())), preferred_element_type=jnp.float32)


def dot_tn(a, b):
    return lax.dot_general(a, b, (((0,), (0,)), ((), ())), preferred_element_type=jnp.float32)


def split(x):
    high = x.astype(jnp.bfloat16)
    return high, (x - high.astype(jnp.float32)).astype(jnp.bfloat16)


def turn_values(shape):
    index = (lax.broadcasted_iota(jnp.int32, shape, 1) + K_LO) % 16
    real = jnp.zeros(shape, jnp.float32)
    imag = jnp.zeros(shape, jnp.float32)
    for i in range(16):
        real = jnp.where(index == i, math.cos(math.pi * i / 8), real)
        imag = jnp.where(index == i, -math.sin(math.pi * i / 8), imag)
    return real, imag


def factors(chan_count, tm_count):
    inner = 2 if chan_count <= 8 else 4
    return {"z": chan_count // inner, "y": inner, "x": tm_count // 2, "c": 2}


def moved(sizes, index, outer, inner, by_outer, by_inner):
    n_outer, n_inner = sizes[outer], sizes[inner]
    hi = lax.rem(lax.div(index, n_inner) + by_outer + n_outer, n_outer)
    lo = lax.rem(lax.rem(index, n_inner) + by_inner + n_inner, n_inner)
    return hi * n_inner + lo


def chan_at(sizes, by_z, by_y):
    return moved(sizes, lax.axis_index("chan"), "z", "y", by_z, by_y)


def tm_at(sizes, by_x, by_c):
    return moved(sizes, lax.axis_index("tm"), "x", "c", by_x, by_c)


def shifted(sizes, value, **by):
    if not any(by.values()):
        return value
    axis, outer, inner = ("chan", "z", "y") if set(by) <= {"z", "y"} else ("tm", "x", "c")
    n_outer, n_inner = sizes[outer], sizes[inner]
    pairs = []
    for index in range(n_outer * n_inner):
        hi = (index // n_inner + by.get(outer, 0)) % n_outer
        lo = (index % n_inner + by.get(inner, 0)) % n_inner
        pairs.append((index, hi * n_inner + lo))
    return lax.ppermute(value, axis, pairs)


def filter_matrix(taps, toeplitz):
    in_index = lax.broadcasted_iota(jnp.int32, (256, 128), 0)
    out_index = lax.broadcasted_iota(jnp.int32, (256, 128), 1)
    tap = in_index - 4 * (out_index % TAPS) - 97
    small = jnp.zeros((256, 128), jnp.float32)
    for j in range(TAPS):
        small = jnp.where(tap == j, taps[0:1, j : j + 1], small)
    slot = lax.broadcasted_iota(jnp.int32, (128, 128), 1) // TAPS
    for a in range(FIR_IN // 128):
        for n in range(FIR_OUT // 128):
            here = jnp.where(slot + n * (128 // TAPS) == a, small[:128], 0.0)
            here = jnp.where(slot + n * (128 // TAPS) == a - 1, small[128:], here)
            toeplitz[a * 128 : (a + 1) * 128, n * 128 : (n + 1) * 128] = here.astype(jnp.bfloat16)


def fir_kernel(x_hbm, fir_hbm, out_ref, x_ref, fir_ref, toeplitz, sems, *, windows):
    chans = x_ref.shape[0] // windows
    fetch_fir = pltpu.make_async_copy(fir_hbm, fir_ref, sems.at[windows])
    fetch_fir.start()
    fetches = []
    for w in range(windows):
        mine = pl.ds(w * chans, chans)
        fetches.append(pltpu.make_async_copy(x_hbm.at[mine], x_ref.at[mine], sems.at[w]))
    fetches[0].start()
    fetch_fir.wait()
    filter_matrix(fir_ref[...].astype(jnp.float32), toeplitz)
    step = 4 * FIR_OUT
    per = SUB // FIR_OUT
    together = 4

    def work(pieces, mine, first):
        piece = dot(jnp.concatenate(pieces, axis=0), toeplitz[...])
        high, low = split(piece)
        for n in range(together):
            i = (first + n) // per
            at = (n % per) * FIR_OUT
            part = slice(n * chans, (n + 1) * chans)
            out_ref[i, mine, at : at + FIR_OUT] = high[part]
            out_ref[i, mine, SUB + at : SUB + at + FIR_OUT] = low[part]
            out_ref[i, mine, 2 * SUB + at : 2 * SUB + at + FIR_OUT] = high[part]

    for w in range(windows):
        mine = slice(w * chans, (w + 1) * chans)
        fetches[w].wait()
        if w + 1 < windows:
            fetches[w + 1].start()
        pieces = [jnp.concatenate([jnp.zeros((chans, 128), jnp.bfloat16), x_ref[mine, :step]], axis=1)]
        for n in range(1, together):
            pieces.append(x_ref[mine, n * step - 128 : (n + 1) * step])
        work(pieces, mine, 0)

        def body(j, carry, mine=mine):
            pieces = []
            for n in range(together):
                first = pl.multiple_of((j * together + n) * step - 128, 128)
                pieces.append(x_ref[mine, pl.ds(first, step + 128)])
            work(pieces, mine, j * together)
            return carry

        lax.fori_loop(1, WIN // FIR_OUT // together, body, 0)


def whiten_kernel(part_ref, *refs, windows, sizes):
    tm_count = sizes["x"] * sizes["c"]
    bins_out = refs[: sizes["z"]]
    rows_out = refs[sizes["z"] : sizes["z"] + tm_count]
    bins_ref, rows_ref = refs[sizes["z"] + tm_count :]
    blocks, rows, _ = part_ref.shape
    chans = rows // windows
    width = bins_ref.shape[2]
    own = rows_ref.shape[2]
    quarters = NFREQ // 128
    turn_re, turn_im = turn_values((1, NFREQ))
    band_a = lax.broadcasted_iota(jnp.int32, (128, 128), 0) // BANDW
    band_b = lax.broadcasted_iota(jnp.int32, (128, 128), 1) // BANDW
    same_band = (band_a == band_b).astype(jnp.bfloat16)
    src = lax.broadcasted_iota(jnp.int32, (256, 256), 0)
    dst = lax.broadcasted_iota(jnp.int32, (256, 256), 1)
    wanted = (dst // (2 * GROUP)) * GROUP + dst % GROUP + 128 * ((dst // GROUP) % 2)
    order = (src == wanted).astype(jnp.bfloat16)
    for w in range(windows):
        mine = slice(w * chans, (w + 1) * chans)
        real = part_ref[blocks - 1, mine, :NFREQ]
        imag = part_ref[blocks - 1, mine, NFREQ:]
        for i in reversed(range(blocks - 1)):
            real, imag = (
                part_ref[i, mine, :NFREQ] + real * turn_re - imag * turn_im,
                part_ref[i, mine, NFREQ:] + real * turn_im + imag * turn_re,
            )
        re = jnp.concatenate([real[:, q * 128 : (q + 1) * 128] for q in range(quarters)], axis=0)
        im = jnp.concatenate([imag[:, q * 128 : (q + 1) * 128] for q in range(quarters)], axis=0)
        power = re * re + im * im
        p0, p1 = split(power)
        p2 = (power - p0.astype(jnp.float32) - p1.astype(jnp.float32)).astype(jnp.bfloat16)
        total = dot(jnp.concatenate([p0, p1, p2], axis=1), jnp.concatenate([same_band] * 3, axis=0))
        gain = lax.rsqrt(total * (1.0 / BANDW) + 1e-06)
        both = jnp.concatenate(
            [(re * gain).astype(jnp.bfloat16), (im * gain).astype(jnp.bfloat16)], axis=1
        )
        both = dot(both, order).astype(jnp.bfloat16)
        for q in range(quarters):
            part = both[q * chans : (q + 1) * chans]
            for n in range(max(1, 256 // width)):
                bins_ref[q * 256 // width + n, mine] = part[:, n * width : (n + 1) * width]
            for t in range(tm_count):
                rows_ref[t, w, :, q * 256 : (q + 1) * 256] = part[t * own : (t + 1) * own]
    for z in range(sizes["z"]):
        for y in range(sizes["y"]):
            bins_out[z][y] = bins_ref[chan_at(sizes, z, y)]
    for x in range(sizes["x"]):
        for c in range(sizes["c"]):
            rows_out[x * sizes["c"] + c][...] = rows_ref[tm_at(sizes, x, c)]


def whitened_spectra(strain, taps, sizes):
    chans, windows, samples = strain.shape
    rows = chans * windows
    chan_count = sizes["z"] * sizes["y"]
    tm_count = sizes["x"] * sizes["c"]
    width = SPEC // chan_count
    own = chans // tm_count
    x = jnp.transpose(strain, (1, 0, 2)).reshape(rows, samples)
    blocks = WIN // SUB
    filtered = pl.pallas_call(
        functools.partial(fir_kernel, windows=windows),
        in_specs=[pl.BlockSpec(memory_space=pl.ANY)] * 2,
        out_shape=jax.ShapeDtypeStruct((blocks, rows, 3 * SUB), jnp.bfloat16),
        scratch_shapes=[
            pltpu.VMEM((rows, samples), jnp.bfloat16),
            pltpu.VMEM((1, TAPS), jnp.bfloat16),
            pltpu.VMEM((FIR_IN, FIR_OUT), jnp.bfloat16),
            pltpu.SemaphoreType.DMA((windows + 1,)),
        ],
        compiler_params=pltpu.CompilerParams(vmem_limit_bytes=46 * MIB),
        name="fir",
    )(x, taps.reshape(1, TAPS))
    part = dot(filtered.reshape(blocks * rows, 3 * SUB), jnp.asarray(forward_constants()))
    outs = pl.pallas_call(
        functools.partial(whiten_kernel, windows=windows, sizes=sizes),
        out_shape=[jax.ShapeDtypeStruct((sizes["y"], rows, width), jnp.bfloat16)] * sizes["z"]
        + [jax.ShapeDtypeStruct((windows, own, SPEC), jnp.bfloat16)] * tm_count,
        scratch_shapes=[
            pltpu.VMEM((chan_count, rows, width), jnp.bfloat16),
            pltpu.VMEM((tm_count, windows, own, SPEC), jnp.bfloat16),
        ],
        compiler_params=pltpu.CompilerParams(vmem_limit_bytes=24 * MIB),
        name="whiten",
    )(part.reshape(blocks, rows, SPEC))
    return outs[: sizes["z"]], outs[sizes["z"] :]


def pick_kernel(channels_ref, *refs, windows, sizes):
    bins = refs[: sizes["z"]]
    outs = refs[sizes["z"] :]
    chans = bins[0].shape[1] // windows
    sources = channels_ref.shape[1]
    chosen = []
    for z in range(sizes["z"]):
        first = chan_at(sizes, -z, 0) * chans
        ids = lax.broadcasted_iota(jnp.int32, (chans, sources), 0) + first
        chosen.append((ids == channels_ref[...]).astype(jnp.bfloat16))
    chosen = jnp.concatenate(chosen, axis=0)
    for y in range(sizes["y"]):
        for w in range(windows):
            block = jnp.concatenate([b[y, w * chans : (w + 1) * chans, :] for b in bins], axis=0)
            outs[y][0, w] = dot_tn(block, chosen).astype(jnp.bfloat16)


def picked_sources(source_channels, bins, windows, sizes):
    sources = source_channels.shape[0]
    width = bins[0].shape[2]
    shape = (1, windows, width, sources)
    parts = pl.pallas_call(
        functools.partial(pick_kernel, windows=windows, sizes=sizes),
        out_shape=[jax.ShapeDtypeStruct(shape, jnp.bfloat16)] * sizes["y"],
        compiler_params=pltpu.CompilerParams(vmem_limit_bytes=16 * MIB),
        name="pick",
    )(source_channels.reshape(1, sources), *bins)
    total = parts[0]
    for y in range(1, sizes["y"]):
        total = total + shifted(sizes, parts[y], y=y)
    return total


def block_at(sizes, step, sign):
    if sizes is None:
        return step
    z = lax.div(step, sizes["y"])
    y = lax.rem(step, sizes["y"])
    return chan_at(sizes, sign * z, sign * y)


def expand_kernel(*refs, sizes):
    out_ref = refs[-1]
    windows, own, _ = refs[0].shape
    depth = windows * (len(refs) - 1) * 2 * GROUP
    groups = 128 // (2 * GROUP)
    lane = lax.broadcasted_iota(jnp.int32, (own, 128), 1)
    first = lane % (2 * GROUP) < GROUP
    bin_row = lax.broadcasted_iota(jnp.int32, (own, GROUP, depth), 1)
    bin_lane = lax.broadcasted_iota(jnp.int32, (own, GROUP, depth), 2) % GROUP
    same = bin_row == bin_lane

    def body(step, carry):
        lanes = pl.ds(pl.multiple_of(block_at(sizes, step, -1) * 128, 128), 128)
        plain = []
        swapped = []
        for ref in refs[:-1]:
            for w in range(windows):
                x = ref[w, :, lanes].astype(jnp.float32)
                plain.append(x)
                ahead = pltpu.roll(x, 128 - GROUP, 1)
                behind = pltpu.roll(x, GROUP, 1)
                swapped.append(jnp.where(first, -ahead, behind))
        for g in range(groups):
            at = slice(g * 2 * GROUP, (g + 1) * 2 * GROUP)
            for p, parts in enumerate((plain, swapped)):
                a = jnp.concatenate([x[:, at] for x in parts], axis=1)
                full = jnp.where(same, a[:, None, :], 0.0)
                out_ref[step * groups + g, :, p * GROUP : (p + 1) * GROUP, :] = full.astype(jnp.bfloat16)
        return carry

    lax.fori_loop(0, SPEC // 128, body, 0)


def expanded_local(local, sizes):
    windows, own, _ = local[0].shape
    depth = windows * len(local) * 2 * GROUP
    out = pl.pallas_call(
        functools.partial(expand_kernel, sizes=sizes),
        out_shape=jax.ShapeDtypeStruct((SPEC // (2 * GROUP), own, 2 * GROUP, depth), jnp.bfloat16),
        cost_estimate=pl.CostEstimate(flops=4 * 10**9, bytes_accessed=8 * MIB, transcendentals=0),
        compiler_params=pltpu.CompilerParams(vmem_limit_bytes=24 * MIB),
        name="expand",
    )(*local)
    return out.reshape(SPEC // (2 * GROUP), own * 2 * GROUP, depth)


def cross_kernel(local_ref, *refs, fetch, own, sizes, by_y):
    sources = refs[:-1]
    out_ref = refs[-1]
    count = sources[0].shape[-1]
    groups = 128 // (2 * GROUP)
    row = lax.broadcasted_iota(jnp.int32, (count, count), 0)
    column = lax.broadcasted_iota(jnp.int32, (count, count), 1)
    identity = (row == column).astype(jnp.bfloat16)

    def body(index, carry):
        step = index if by_y is None else index * sizes["y"] + by_y
        tiles = fetch(sources, step)
        cross = []
        for g in range(groups):
            rows = slice(g * 2 * GROUP, (g + 1) * 2 * GROUP)
            block = jnp.concatenate([tile[rows] for tile in tiles], axis=0)
            cross.append(dot(local_ref[step * groups + g], block).astype(jnp.bfloat16))
        tall = jnp.concatenate(
            [x[c * 2 * GROUP : (c + 1) * 2 * GROUP] for c in range(own) for x in cross], axis=0
        )
        turned = dot_nt(identity, tall)
        by_channel = jnp.stack([turned[:, c * 128 : (c + 1) * 128] for c in range(own)], axis=0)
        mixed = jnp.transpose(by_channel, (1, 0, 2)).reshape(count * own, 128)
        block = step if sizes is None else lax.div(block_at(sizes, step, -1), sizes["y"])
        out_ref[:, pl.ds(pl.multiple_of(block * 128, 128), 128)] = mixed.astype(jnp.bfloat16)
        return carry

    lax.fori_loop(0, SPEC // 128 if by_y is None else sizes["z"], body, 0)


def crossed(local, sources, fetch, sizes, by_y=None):
    _, expanded_rows, _ = local.shape
    own = expanded_rows // (2 * GROUP)
    count = sources[0].shape[-1]
    columns = SPEC if by_y is None else 128 * sizes["z"]
    return pl.pallas_call(
        functools.partial(cross_kernel, fetch=fetch, own=own, sizes=sizes, by_y=by_y),
        out_shape=jax.ShapeDtypeStruct((count * own, columns), jnp.bfloat16),
        cost_estimate=pl.CostEstimate(flops=4 * 10**9, bytes_accessed=8 * MIB, transcendentals=0),
        compiler_params=pltpu.CompilerParams(vmem_limit_bytes=32 * MIB),
        name="cross",
    )(local, *sources)


def table_rows(table_ref, columns, sizes, by_y):
    if by_y is None:
        return table_ref[...]
    y = lax.rem(chan_at(sizes, 0, -by_y), sizes["y"])
    rows = [pl.ds(pl.multiple_of((z * sizes["y"] + y) * 128, 128), 128) for z in range(columns // 128)]
    return jnp.concatenate([table_ref[r] for r in rows], axis=0)


def part_kernel(cross_ref, table_ref, out_ref, chosen, *, sizes, by_y):
    chosen[...] = table_rows(table_ref, cross_ref.shape[1], sizes, by_y)
    height = 512

    def body(i, carry):
        mine = pl.ds(pl.multiple_of(i * height, height), height)
        rows = cross_ref[mine]
        for n in range(LAGS // 256):
            at = slice(n * 256, (n + 1) * 256)
            out_ref[mine, at] = dot(rows, chosen[:, at])
        return carry

    lax.fori_loop(0, cross_ref.shape[0] // height, body, 0)


def lag_kernel(*refs, scale, sizes, by_y):
    cross_ref, table_ref = refs[:2]
    chosen, buffer, sems = refs[-3:]
    out_hbm = refs[-4]
    earlier = refs[2:-4]
    depth, height, lags = buffer.shape
    steps = cross_ref.shape[0] // height
    chosen[...] = table_rows(table_ref, cross_ref.shape[1], sizes, by_y)

    def store(i):
        mine = pl.ds(pl.multiple_of(i * height, height), height)
        slot = lax.rem(i, depth)
        return pltpu.make_async_copy(buffer.at[slot], out_hbm.at[mine], sems.at[slot])

    def body(i, carry):
        @pl.when(i >= depth)
        def _():
            store(i - depth).wait()

        mine = pl.ds(pl.multiple_of(i * height, height), height)
        rows = cross_ref[mine]
        slot = lax.rem(i, depth)
        for n in range(lags // 256):
            at = slice(n * 256, (n + 1) * 256)
            total = dot(rows, chosen[:, at])
            for held in earlier:
                total = total + held[mine, at]
            buffer[slot, :, at] = total * scale
        store(i).start()
        return carry

    lax.fori_loop(0, steps, body, 0)
    for i in range(max(0, steps - depth), steps):
        store(i).wait()


def lag_parts(cross, sizes, by_y):
    rows, columns = cross.shape
    return pl.pallas_call(
        functools.partial(part_kernel, sizes=sizes, by_y=by_y),
        out_shape=jax.ShapeDtypeStruct((rows, LAGS), jnp.float32),
        scratch_shapes=[pltpu.VMEM((columns, LAGS), jnp.bfloat16)],
        cost_estimate=pl.CostEstimate(flops=4 * 10**9, bytes_accessed=8 * MIB, transcendentals=0),
        compiler_params=pltpu.CompilerParams(vmem_limit_bytes=24 * MIB),
        name="lags_near",
    )(cross, jnp.asarray(lag_constant()))


def correlations(cross, earlier, window_total, sizes=None, by_y=None):
    rows, columns = cross.shape
    height = 256
    return pl.pallas_call(
        functools.partial(
            lag_kernel, scale=1.0 / math.sqrt(NFREQ * window_total), sizes=sizes, by_y=by_y
        ),
        in_specs=[pl.BlockSpec(memory_space=pltpu.VMEM)] * (2 + len(earlier)),
        out_specs=pl.BlockSpec(memory_space=pl.ANY),
        out_shape=jax.ShapeDtypeStruct((rows, LAGS), jnp.float32),
        scratch_shapes=[
            pltpu.VMEM((columns, LAGS), jnp.bfloat16),
            pltpu.VMEM((3, height, LAGS), jnp.float32),
            pltpu.SemaphoreType.DMA((3,)),
        ],
        compiler_params=pltpu.CompilerParams(vmem_limit_bytes=24 * MIB),
        name="lags",
    )(cross, jnp.asarray(lag_constant()), *earlier)


def gathered(picked, local, window_total, sizes):
    windows, width = picked.shape[1:3]
    half = width // 2
    whole = jnp.concatenate([shifted(sizes, picked, z=d) for d in range(sizes["z"])], axis=0)
    held = {(0, 0): [whole]}
    for x in range(1, sizes["x"]):
        held[x, 0] = [shifted(sizes, whole, x=x)]
    for y in range(1, sizes["y"]):
        held[0, y] = [shifted(sizes, whole, y=y)]
    expanded = expanded_local(local, sizes)
    edges = {key: array for key, array in held.items() if key != (0, 0)}
    edges, expanded = lax.optimization_barrier((edges, expanded))
    held.update(edges)
    for x in range(1, sizes["x"]):
        for y in range(1, sizes["y"]):
            held[x, y] = [
                shifted(sizes, held[0, y][0][:, :, :half], x=x),
                shifted(sizes, held[x, 0][0][:, :, half:], y=y),
            ]

    def rows_of(y):
        arrays = []
        place = {}
        for x in range(sizes["x"]):
            for c in range(sizes["c"]):
                place[x, c] = len(arrays)
                arrays += [shifted(sizes, array, c=c) for array in held[x, y]]

        def fetch(refs, step):
            by_z = lax.div(step, sizes["y"])
            tiles = []
            for x in range(sizes["x"]):
                for c in range(sizes["c"]):
                    parts = refs[place[x, c] : place[x, c] + len(held[x, y])]
                    for w in range(windows):
                        tiles.append(jnp.concatenate([part[by_z, w] for part in parts], axis=0))
            return tiles

        return arrays, fetch

    earlier = []
    for y in range(sizes["y"]):
        if y > 0:
            far = {key: array for key, array in held.items() if key[0] and key[1]}
            earlier.append(lag_parts(cross, sizes, y - 1))
            far, earlier = lax.optimization_barrier((far, earlier))
            held.update(far)
        arrays, fetch = rows_of(y)
        cross = crossed(expanded, arrays, fetch, sizes, by_y=y)
    return correlations(cross, earlier, window_total, sizes, sizes["y"] - 1)


def gathered_plainly(picked, local, window_total, sizes):
    parts = [shifted(sizes, picked, x=x, c=c) for x in range(sizes["x"]) for c in range(sizes["c"])]
    mine = jnp.concatenate(parts, axis=1)[0]
    total, width, count = mine.shape
    held = lax.all_gather(mine, "chan", axis=0, tiled=False)
    held = held.reshape(SPEC // 128, 128 // width, total, width, count)
    held = jnp.transpose(held, (0, 2, 1, 3, 4)).reshape(SPEC // 128, total, 128, count)

    def fetch(refs, step):
        return [refs[0][step, i] for i in range(total)]

    cross = crossed(expanded_local(local, None), [held], fetch, None)
    return correlations(cross, [], window_total)


def on_device(strain_rate, fir_taps, source_channels):
    sizes = factors(lax.axis_size("chan"), lax.axis_size("tm"))
    windows = strain_rate.shape[1]
    bins, rows = whitened_spectra(strain_rate, fir_taps, sizes)
    bins = [shifted(sizes, b, z=z) for z, b in enumerate(bins)]
    moves = [(x, c) for x in range(sizes["x"]) for c in range(sizes["c"])]
    local = [shifted(sizes, r, x=x, c=c) for r, (x, c) in zip(rows, moves)]
    bins, local = lax.optimization_barrier((bins, local))
    picked = picked_sources(source_channels, bins, windows, sizes)
    gather = gathered if picked.shape[2] == 128 else gathered_plainly
    out = gather(picked, local, windows * lax.axis_size("tm"), sizes)
    return out.reshape(source_channels.shape[0], -1, LAGS)


def solution(mesh):
    placed = (P("chan", "tm", None), P(), P())
    return jax.shard_map(
        on_device,
        mesh=mesh,
        in_specs=placed,
        out_specs=P(None, ("chan", "tm"), None),
        check_vma=False,
    )
```
